512 devices in a mesh: member: 32 (over y_hi, z), lat: 8 (over y_lo, x), lev: 2 (over core).
Axes of the slice: x: 4, y: 4 (y_hi: 2, y_lo: 2; y = y_hi * 2 + y_lo), z: 16, core: 2. Of those that a mesh axis runs over, the one named last changes fastest.
Arguments:
- alpha_field: float32 [32, 8, 640, 1280], P('member', 'lev', 'lat'), may hold values from -1.0606601 to 1.0606601
- perturbation: bfloat16 [32, 8, 640, 1280], P('member', 'lev', 'lat'), may hold values from -6 to 6
- obs_value: float32 [8, 640, 1280], P('lev', 'lat', 'member'), may hold values from -6 to 6
- obs_mask: int32 [8, 640, 1280], P('lev', 'lat', 'member'), may hold values 0 or 1
- obs_precision: float32 [8], P('lev'), may hold values from 0.5 to 2
- loc_width: int32 [8], P('lev'), may hold values from 6 to 24, as said below
Outputs:
- gradient: float32 [32, 8, 640, 1280], P('member', 'lev', 'lat')
- increment: float32 [8, 640, 1280], P('lev', 'lat', 'member')
The draws below stay inside these ranges and needn't reach their ends.
Inputs may be any that keep to these rules, and one draw needn't show every extreme that they name: `loc_width`: one length scale a level; some level has the smallest and some the largest value.
All inputs are finite; a program needn't handle non-finite values. No bound on the sum of `obs_mask` on one device may be relied on, other than what follows from the above.
Results may differ from the reference program's by a relative error of at most 0.0059.
Values may be sent and summed in bfloat16 or wider, within the bound.
A program may use at most 64 MiB of HBM per device.

```python
import math
import jax
import jax.numpy as jnp
from jax import lax

NLON = 1280
HALO = 24
NLAT = 640
LEV = 8
MEMBERS = 32


def draw_loc_width(key, part):
    key = jax.random.fold_in(key, 7)
    first_key, second_key = jax.random.split(key)
    values = jax.random.randint(first_key, (LEV,), 6, 25)
    order = jax.random.permutation(second_key, LEV)
    values = values.at[order[0]].set(6).at[order[1]].set(24)
    return values.astype(jnp.int32)


def plant(result, rng, low, largest):
    longest = result.shape.index(max(result.shape))
    spots = []
    for shift in (0, 1):
        where = [jax.random.randint(jax.random.fold_in(rng, axis), (), 0, length) for axis, length in enumerate(result.shape)]
        where[longest] = (where[longest] + shift) % result.shape[longest]
        spots.append(tuple(where))
    return result.at[spots[0]].set(low).at[spots[1]].set(largest)


def with_spikes(array, key, source, target, parts, factor):
    def block_of(axis_at):
        return (jnp.arange(array.shape[axis_at]) // (array.shape[axis_at] // parts)).reshape((-1,) + (1,) * (array.ndim - 1 - axis_at))

    first = jax.random.permutation(key, parts)[block_of(target)]
    far = (block_of(target) + parts // 2) % parts
    return jnp.where((block_of(source) == first) | (block_of(source) == far), factor * array, array)


def shard_levels(rng, shape, pieces, smallest, high):
    def one(axis_at, blocks):
        steps = jax.random.uniform(jax.random.fold_in(jax.random.fold_in(rng, 6), axis_at), (blocks,), jnp.float32, smallest / len(pieces), high / len(pieces))
        return jnp.repeat(jnp.exp(steps), shape[axis_at] // blocks).reshape((-1,) + (1,) * (len(shape) - axis_at - 1))

    level = one(*pieces[0])
    for cut in pieces[1:]:
        level = level * one(*cut)
    return level


def bell_draw(stream_key, extent, scale, limit, cuts=(), kind=jnp.bfloat16):
    level = shard_levels(stream_key, extent, cuts, -0.22, 0.18) if cuts else 1.0
    result = jax.random.normal(stream_key, extent, jnp.float32) * scale * level
    return jnp.minimum(jnp.maximum(result, -limit), limit).astype(kind)


def heavy_noise(stream_key, extent, scale, limit, pieces, heavy, kind=jnp.bfloat16):
    result = scale * jax.random.normal(stream_key, extent, jnp.float32)
    if pieces:
        result = result * shard_levels(stream_key, extent, pieces, -0.22, 0.18)
    return jnp.clip(with_spikes(result, jax.random.fold_in(stream_key, 3), *heavy), -limit, limit).astype(kind)


def setup_inputs(seed: int = 0) -> dict:
    key_list = jax.random.split(jax.random.key(seed), 7)
    return {
        "alpha_field": bell_draw(key_list[0], (MEMBERS, LEV, NLAT, NLON), (1.0 / MEMBERS ** 0.5), 1.0606601, ((0, 32), (1, 2), (2, 8)), jnp.float32),
        "perturbation": heavy_noise(key_list[1], (MEMBERS, LEV, NLAT, NLON), 1.0, 6.0, ((0, 32), (1, 2), (2, 8)), (0, 3, 32, 2.75)),
        "obs_value": bell_draw(key_list[2], (LEV, NLAT, NLON), 1.0, 6.0, ((0, 2), (1, 8), (2, 32)), jnp.float32),
        "obs_mask": plant((jax.random.randint(key_list[3], (LEV, NLAT, NLON), 0, 2) < 1).astype(jnp.int32), jax.random.fold_in(key_list[3], 1), 0, 1),
        "obs_precision": jnp.clip(jnp.exp(math.log(2.0) - 1.3862944 * jax.random.uniform(key_list[4], (LEV,), jnp.float32) ** shard_levels(key_list[4], (LEV,), ((0, 2),), -0.2, 0.2)), 0.5, 2.0),
        "loc_width": draw_loc_width(jax.random.fold_in(key_list[6], 71), 0),
    }


vert_scale = 2.0

def vertical_matrix(rows, count):
    cols = jnp.arange(count, dtype=jnp.int32)
    diff = (rows[:, None] - cols[None, :]).astype(jnp.float32)
    return 0.5 * jnp.exp(-diff * diff / (2.0 * vert_scale * vert_scale))

def lat_kernel(widths):
    offsets = jnp.arange(-HALO, HALO + 1, dtype=jnp.int32).astype(jnp.float32)
    spread = widths.astype(jnp.float32)[:, None] / 3.0
    weights = jnp.exp(-offsets[None, :] ** 2 / (2.0 * spread ** 2))
    norm_sq = lax.optimization_barrier(jnp.sum(jnp.exp(-offsets[None, :] ** 2 / spread ** 2), axis=1, keepdims=True))
    return weights / jnp.sqrt(norm_sq)

def lon_table(width, count):
    rows = jnp.arange(count, dtype=jnp.int32)
    diff = jnp.abs(rows[:, None] - rows[None, :])
    dist = jnp.minimum(diff, count - diff).astype(jnp.float32)
    cycle_dist = jnp.minimum(rows, count - rows).astype(jnp.float32)
    scale = width.astype(jnp.float32)
    norm_sq = jnp.sum(jnp.exp(-cycle_dist ** 2 / scale ** 2))
    return (jnp.exp(-dist ** 2 / (2.0 * scale ** 2)) / jnp.sqrt(norm_sq)).astype(jnp.bfloat16)

def lat_apply(padded, kernel, band):
    total = jnp.zeros((padded.shape[0], band, padded.shape[2]), jnp.float32)
    for offset in range(2 * HALO + 1):
        total = total + kernel[:, offset, None, None] * padded[:, offset:offset + band].astype(jnp.float32)
    return total

def reference(alpha_field, perturbation, obs_value, obs_mask, obs_precision, loc_width):
    kernel = lat_kernel(loc_width)
    tables = jax.vmap(lambda width: lon_table(width, NLON))(loc_width).astype(jnp.float32)
    mixing = vertical_matrix(jnp.arange(LEV, dtype=jnp.int32), LEV)

    def forward(total, pair):
        field, member_pert = pair
        rounded = lax.optimization_barrier(field.astype(jnp.bfloat16)).astype(jnp.float32)
        vertical = jnp.einsum('ij,jrn->irn', mixing, rounded, precision=lax.Precision.HIGHEST)
        vertical_b = vertical.astype(jnp.bfloat16)
        padded = jnp.pad(vertical_b, ((0, 0), (HALO, HALO), (0, 0)))
        smoothed = lat_apply(padded, kernel, NLAT)
        smooth_b = lax.optimization_barrier(smoothed.astype(jnp.bfloat16)).astype(jnp.float32)
        spread_field = jnp.einsum('lrn,lnm->lrm', smooth_b, tables)
        return (total + member_pert.astype(jnp.float32) * spread_field, None)
    start = jnp.zeros((LEV, NLAT, NLON), jnp.float32)
    increment, _ = lax.scan(forward, start, (alpha_field, perturbation))
    weighted = obs_mask.astype(jnp.float32) * obs_precision[:, None, None]
    adjoint_b = (weighted * (increment - obs_value)).astype(jnp.bfloat16)

    def backward(pair):
        field, member_pert = pair
        product = member_pert.astype(jnp.float32) * adjoint_b.astype(jnp.float32)
        product_b = lax.optimization_barrier(product.astype(jnp.bfloat16)).astype(jnp.float32)
        along = jnp.einsum('lrn,lnm->lrm', product_b, tables).astype(jnp.bfloat16)
        padded = jnp.pad(along, ((0, 0), (HALO, HALO), (0, 0)))
        smoothed = lat_apply(padded, kernel, NLAT)
        smooth_b = lax.optimization_barrier(smoothed.astype(jnp.bfloat16)).astype(jnp.float32)
        return field + jnp.einsum('ij,jrn->irn', mixing, smooth_b, precision=lax.Precision.HIGHEST)
    gradient = lax.map(backward, (alpha_field, perturbation))
    return (gradient, increment)
```

```python
import functools
import math

import jax
import jax.numpy as jnp
from jax import lax
from jax.experimental import pallas as pl
from jax.experimental.pallas import tpu as pltpu
from jax.sharding import PartitionSpec as P

HALO = 24
GROUPS = 2
BLOCK = 256
VERT_SCALE = 2.0
F32 = jnp.float32
BF16 = jnp.bfloat16
MESH = pl.DeviceIdType.MESH


def vert_weight(diff):
    return 0.5 * math.exp(-diff * diff / (2.0 * VERT_SCALE * VERT_SCALE))


def kernel(
    ring, lat_count, lev_count,
    alpha, pert, obs, mask, prec, width,
    grad, inc,
    own, far, band, edge_f, edge, halo, latk, table, rolled, flat, turned,
    run_tx, run_rx, pair_tx, pair_rx, site, total, adj, back, back_far,
    lev_send, lev_recv, halo_send, halo_recv, site_send, site_recv,
    run_send, run_recv, pair_send, pair_recv, gather_send, gather_recv,
):
    levels, rows, cols = alpha.shape
    blocks = cols // BLOCK
    cell = cols // (ring * GROUPS)
    half = ring // 2
    pad = flat.shape[0]
    used = levels * rows

    member = lax.axis_index("member")
    lat = lax.axis_index("lat")
    lev = lax.axis_index("lev")
    z = lax.rem(member, ring)
    group = lax.div(member, ring)

    def at_z(index):
        return {"member": group * ring + lax.rem(index + ring, ring)}

    after, before = at_z(z + 1), at_z(z - 1)
    pair = {"member": lax.rem(member + ring, ring * GROUPS)}
    south = {"lat": lax.rem(lat + 1, lat_count)}
    north = {"lat": lax.rem(lat + lat_count - 1, lat_count)}
    sibling = {"lev": 1 - lev}

    def remote(src, dst, send, recv, to):
        return pltpu.make_async_remote_copy(
            src_ref=src, dst_ref=dst, send_sem=send, recv_sem=recv, device_id=to, device_id_type=MESH
        )

    def lev_copy(phase, level):
        src, dst = ((own, far), (back, back_far))[phase]
        return remote(src.at[level], dst.at[level], lev_send.at[phase, level], lev_recv.at[phase, level], sibling)

    def halo_copy(phase, side):
        return remote(
            edge.at[phase, side], halo.at[phase, 1 - side],
            halo_send.at[phase, side], halo_recv.at[phase, 1 - side], (north, south)[side],
        )

    def site_copy():
        return remote(site.at[group], site.at[group], site_send, site_recv, pair)

    def site_arrival():
        return remote(site.at[1 - group], site.at[1 - group], site_send, site_recv, pair)

    def run_copy(way, step):
        return remote(
            run_tx.at[way, step], run_rx.at[way, step],
            run_send.at[way, step], run_recv.at[way, step], (after, before)[way],
        )

    def pair_copy():
        return remote(pair_tx, pair_rx, pair_send, pair_recv, pair)

    def origin(way, step):
        return lax.rem(z + (ring - step if way == 0 else step), ring)

    def gather_copy(way, step):
        chunk = origin(way, step)
        return remote(
            adj.at[chunk], adj.at[chunk], gather_send.at[way, step], gather_recv.at[way, step], (after, before)[way]
        )

    def gather_arrival(way, step):
        chunk = origin(way, step + 1)
        return remote(
            adj.at[chunk], adj.at[chunk], gather_send.at[way, step], gather_recv.at[way, step], (after, before)[way]
        )

    barrier = pltpu.get_barrier_semaphore()
    partners = (after, before, pair, south, north, sibling)
    for partner in partners:
        pl.semaphore_signal(barrier, inc=1, device_id=partner, device_id_type=MESH)

    def round_level(level, carry):
        own[level] = alpha[level].astype(BF16)
        return carry

    lax.fori_loop(0, levels, round_level, 0)

    site[group] = jnp.zeros(site.shape[1:], F32)
    for level in range(levels):
        lanes = slice(level * rows, (level + 1) * rows)
        site[group, 0, :, lanes] = obs[level]
        site[group, 1, :, lanes] = mask[level].astype(F32) * prec[level]
    pl.semaphore_wait(barrier, len(partners))

    for level in range(levels):
        lev_copy(0, level).start()
    site_copy().start()

    def build_latk(level, carry):
        scale = jnp.full((1, 128), width[level].astype(F32), F32) / 3.0
        lane = lax.broadcasted_iota(jnp.int32, (1, 128), 1)
        step = (lane - HALO).astype(F32)
        norm_sq = jnp.sum(
            jnp.where(lane <= 2 * HALO, jnp.exp(-(step * step) / (scale * scale)), 0.0), axis=1, keepdims=True
        )
        row = lax.broadcasted_iota(jnp.int32, (rows, 128), 0)
        col = lax.broadcasted_iota(jnp.int32, (rows, 128), 1)
        is_top = jnp.logical_and(col >= rows, col < rows + HALO)
        is_bottom = col >= rows + HALO
        place = jnp.where(is_top, col - rows - HALO, col)
        place = jnp.where(is_bottom, col - HALO, place)
        diff = place - row
        keep = jnp.abs(diff) <= HALO
        keep = jnp.logical_and(keep, jnp.logical_or(jnp.logical_not(is_top), lat > 0))
        keep = jnp.logical_and(keep, jnp.logical_or(jnp.logical_not(is_bottom), lat < lat_count - 1))
        dist = diff.astype(F32)
        weight = jnp.exp(-(dist * dist) / (2.0 * scale * scale)) / jnp.sqrt(norm_sq)
        weight = jnp.where(keep, weight, 0.0)
        high = weight.astype(BF16)
        latk[level, 0:rows] = high
        latk[level, rows : 2 * rows] = (weight - high.astype(F32)).astype(BF16)
        return carry

    lax.fori_loop(0, levels, build_latk, 0)

    def build_table(level, carry):
        scale = jnp.full((1, 128), width[level].astype(F32), F32)[:, 0:1]
        square = scale * scale
        place = lax.broadcasted_iota(jnp.int32, (1, cols), 1)
        cycle = jnp.minimum(place, cols - place).astype(F32)
        norm_sq = jnp.sum(jnp.exp(-(cycle * cycle) / square), axis=1, keepdims=True)
        inverse = 1.0 / jnp.sqrt(norm_sq)
        factor = -1.0 / (2.0 * square)
        chunk = 64

        def some(index, inner):
            row = lax.broadcasted_iota(jnp.int32, (chunk, BLOCK), 0) + index * chunk
            col = lax.broadcasted_iota(jnp.int32, (chunk, BLOCK), 1)
            diff = jnp.abs(row - col)
            dist = jnp.minimum(diff, cols - diff).astype(F32)
            table[level, pl.ds(pl.multiple_of(index * chunk, chunk), chunk)] = (
                jnp.exp(dist * dist * factor) * inverse
            ).astype(BF16)
            return inner

        return lax.fori_loop(0, cols // chunk, some, carry)

    near_weights = [[vert_weight(i - j) for j in range(levels)] for i in range(levels)]
    far_weights = [
        [
            jnp.where(lev == 0, jnp.float32(vert_weight(i - j - levels)), jnp.float32(vert_weight(i - j + levels)))
            for j in range(levels)
        ]
        for i in range(levels)
    ]

    def vertical(near, remote_levels, emit):
        def lane_block(block, carry):
            lanes = pl.ds(pl.multiple_of(block * BLOCK, BLOCK), BLOCK)
            for chunk in range(rows // 16):
                part = slice(16 * chunk, 16 * chunk + 16)
                a = [near[j, part, lanes].astype(F32) for j in range(levels)]
                b = [remote_levels[j, part, lanes].astype(F32) for j in range(levels)]
                for i in range(levels):
                    value = near_weights[i][0] * a[0]
                    for j in range(1, levels):
                        value = value + near_weights[i][j] * a[j]
                    for j in range(levels):
                        value = value + far_weights[i][j] * b[j]
                    emit(i, chunk, part, lanes, value)
            return carry

        lax.fori_loop(0, blocks, lane_block, 0)

    def emit_forward(i, chunk, part, lanes, value):
        band[i, part, lanes] = value.astype(BF16)
        first = 16 * chunk
        top = min(HALO, first + 16) - first
        if top > 0:
            edge_f[0, HALO * i + first : HALO * i + first + top, lanes] = value[0:top]
        skip = max(0, rows - HALO - first)
        if skip < 16:
            start = HALO * i + first + skip - (rows - HALO)
            edge_f[1, start : start + 16 - skip, lanes] = value[skip:16]

    for level in range(levels):
        lev_copy(0, level).wait_recv()
    vertical(own, far, emit_forward)

    def send_edges(phase):
        def lane_block(block, carry):
            lanes = pl.ds(pl.multiple_of(block * BLOCK, BLOCK), BLOCK)
            for side in range(2):
                edge[phase, side, :, lanes] = edge_f[side, :, lanes].astype(BF16)
            return carry

        lax.fori_loop(0, blocks, lane_block, 0)
        for side in range(2):
            halo_copy(phase, side).start()

    def receive_edges(phase):
        for side in range(2):
            halo_copy(phase, side).wait_recv()

        def lane_block(block, carry):
            lanes = pl.ds(pl.multiple_of(block * BLOCK, BLOCK), BLOCK)
            top = halo[phase, 0, :, lanes].astype(F32)
            bottom = halo[phase, 1, :, lanes].astype(F32)
            for i in range(levels):
                part = slice(HALO * i, HALO * i + HALO)
                band[i, rows : rows + 2 * HALO, lanes] = jnp.concatenate([top[part], bottom[part]], axis=0).astype(BF16)
            return carry

        lax.fori_loop(0, blocks, lane_block, 0)

    def smooth(level, block):
        both = jnp.dot(latk[level], band[level, :, block * BLOCK : (block + 1) * BLOCK], preferred_element_type=F32)
        return (both[0:rows] + both[rows : 2 * rows]).astype(BF16)

    def spread_out(block, value):
        for turn in range(blocks):
            start = ((block - turn) % blocks) * BLOCK
            rolled[turn * rows : (turn + 1) * rows, start : start + BLOCK] = value

    def along_longitude(level):
        return jnp.dot(rolled[...], table[level], preferred_element_type=F32)

    send_edges(0)
    lax.fori_loop(0, levels, build_table, 0)
    flat[used:pad] = jnp.zeros((pad - used, cols), F32)
    receive_edges(0)

    def forward(level, carry):
        for block in range(blocks):
            spread_out(block, smooth(level, block))
        out = along_longitude(level)
        here = pl.ds(pl.multiple_of(level * rows, 16), rows)
        for block in range(blocks):
            lanes = slice(block * BLOCK, (block + 1) * BLOCK)
            flat[here, lanes] = out[block * rows : (block + 1) * rows] * pert[level, :, lanes].astype(F32)
        return carry

    lax.fori_loop(0, levels, forward, 0)

    def turn_forward(index, carry):
        part = pl.ds(pl.multiple_of(index * 128, 128), 128)
        turned[part, :] = flat[:, part].T
        return carry

    lax.fori_loop(0, cols // 128, turn_forward, 0)

    def split_rows(chunk):
        return [pl.ds(pl.multiple_of(g * (cols // GROUPS) + chunk * cell, 8), cell) for g in range(GROUPS)]

    def term(chunk):
        return jnp.concatenate([turned[part, :] for part in split_rows(chunk)], axis=0)

    def target(way, step):
        return lax.rem(z + (half - step if way == 0 else half + 1 + step), ring)

    for way in range(2):
        run_tx[way, 0] = term(target(way, 0)).astype(BF16)
        run_copy(way, 0).start()

    def hop(way, step):
        run_copy(way, step - 1).wait_recv()
        run_tx[way, step] = (run_rx[way, step - 1].astype(F32) + term(target(way, step))).astype(BF16)
        run_copy(way, step).start()

    def hops(step, carry):
        for way in range(2):
            hop(way, step)
        return carry

    lax.fori_loop(1, half - 1, hops, 0)
    hop(0, half - 1)
    run_copy(1, half - 2).wait_recv()
    mine = term(z) + run_rx[1, half - 2].astype(F32)
    run_copy(0, half - 1).wait_recv()
    mine = mine + run_rx[0, half - 1].astype(F32)
    total[...] = mine
    pair_tx[...] = mine.astype(BF16)
    pair_copy().start()
    site_arrival().wait_recv()
    pair_copy().wait_recv()
    summed = total[...] + pair_rx[...].astype(F32)
    total[...] = summed
    seen = jnp.concatenate([site[g, 0] for g in range(GROUPS)], axis=0)
    weight = jnp.concatenate([site[g, 1] for g in range(GROUPS)], axis=0)
    adj[z] = (weight * (summed - seen)).astype(BF16)

    for way in range(2):
        gather_copy(way, 0).start()

    def unpack(chunk):
        value = adj[chunk].astype(F32)
        for g, part in enumerate(split_rows(chunk)):
            turned[part, :] = value[g * cell : (g + 1) * cell]

    unpack(z)
    result = total[pl.ds(pl.multiple_of(group * cell, 8), cell), :]
    for level in range(levels):
        inc[level] = result[:, level * rows : (level + 1) * rows]

    def pass_on(way, step):
        gather_arrival(way, step - 1).wait_recv()
        gather_copy(way, step).start()
        unpack(origin(way, step))

    def passes(step, carry):
        for way in range(2):
            pass_on(way, step)
        return carry

    lax.fori_loop(1, half - 1, passes, 0)
    pass_on(0, half - 1)
    gather_arrival(1, half - 2).wait_recv()
    unpack(origin(1, half - 1))
    gather_arrival(0, half - 1).wait_recv()
    unpack(origin(0, half))

    def turn_back(index, carry):
        part = pl.ds(pl.multiple_of(index * 128, 128), 128)
        flat[:, part] = turned[part, :].T
        return carry

    lax.fori_loop(0, cols // 128, turn_back, 0)

    def backward(level, carry):
        here = pl.ds(pl.multiple_of(level * rows, 16), rows)
        for block in range(blocks):
            lanes = slice(block * BLOCK, (block + 1) * BLOCK)
            spread_out(block, (flat[here, lanes] * pert[level, :, lanes].astype(F32)).astype(BF16))
        out = along_longitude(level)
        reach = pl.ds(pl.multiple_of(level * HALO, 8), HALO)
        for block in range(blocks):
            lanes = slice(block * BLOCK, (block + 1) * BLOCK)
            value = out[block * rows : (block + 1) * rows]
            band[level, 0:rows, lanes] = value.astype(BF16)
            edge_f[0, reach, lanes] = value[0:HALO]
            edge_f[1, reach, lanes] = value[rows - HALO : rows]
        return carry

    lax.fori_loop(0, levels, backward, 0)
    send_edges(1)
    receive_edges(1)

    def smooth_back(level, carry):
        for block in range(blocks):
            back[level, :, block * BLOCK : (block + 1) * BLOCK] = smooth(level, block)
        lev_copy(1, level).start()
        return carry

    lax.fori_loop(0, levels, smooth_back, 0)

    def emit_back(i, chunk, part, lanes, value):
        grad[i, part, lanes] = alpha[i, part, lanes] + value

    for level in range(levels):
        lev_copy(1, level).wait_recv()
    vertical(back, back_far, emit_back)

    for phase in range(2):
        for level in range(levels):
            lev_copy(phase, level).wait_send()
        for side in range(2):
            halo_copy(phase, side).wait_send()
    site_copy().wait_send()
    pair_copy().wait_send()

    def drain(step, carry):
        for way in range(2):
            run_copy(way, step).wait_send()
            gather_copy(way, step).wait_send()
        return carry

    lax.fori_loop(0, half - 1, drain, 0)
    run_copy(0, half - 1).wait_send()
    gather_copy(0, half - 1).wait_send()


def solution(mesh):
    ring = mesh.shape["member"] // GROUPS
    lat_count, lev_count = mesh.shape["lat"], mesh.shape["lev"]

    def body(alpha_field, perturbation, obs_value, obs_mask, obs_precision, loc_width):
        _, levels, rows, cols = alpha_field.shape
        cell = obs_value.shape[2]
        used = levels * rows
        pad = -(-used // 128) * 128
        chunk = GROUPS * cell
        half = ring // 2
        vmem = pl.BlockSpec(memory_space=pltpu.VMEM)
        smem = pl.BlockSpec(memory_space=pltpu.SMEM)
        dma = pltpu.SemaphoreType.DMA
        full = (levels, rows, cols)
        gradient, increment = pl.pallas_call(
            functools.partial(kernel, ring, lat_count, lev_count),
            out_shape=(
                jax.ShapeDtypeStruct(full, F32),
                jax.ShapeDtypeStruct((levels, cell, rows), F32),
            ),
            in_specs=[vmem, vmem, vmem, vmem, smem, smem],
            out_specs=(vmem, vmem),
            scratch_shapes=[
                pltpu.VMEM(full, BF16),
                pltpu.VMEM(full, BF16),
                pltpu.VMEM((levels, rows + 2 * HALO, cols), BF16),
                pltpu.VMEM((2, levels * HALO, cols), F32),
                pltpu.VMEM((2, 2, levels * HALO, cols), BF16),
                pltpu.VMEM((2, 2, levels * HALO, cols), BF16),
                pltpu.VMEM((levels, 2 * rows, rows + 2 * HALO), BF16),
                pltpu.VMEM((levels, cols, BLOCK), BF16),
                pltpu.VMEM((cols // BLOCK * rows, cols), BF16),
                pltpu.VMEM((pad, cols), F32),
                pltpu.VMEM((cols, pad), F32),
                pltpu.VMEM((2, half, chunk, pad), BF16),
                pltpu.VMEM((2, half, chunk, pad), BF16),
                pltpu.VMEM((chunk, pad), BF16),
                pltpu.VMEM((chunk, pad), BF16),
                pltpu.VMEM((GROUPS, 2, cell, pad), F32),
                pltpu.VMEM((chunk, pad), F32),
                pltpu.VMEM((ring, chunk, pad), BF16),
                pltpu.VMEM(full, BF16),
                pltpu.VMEM(full, BF16),
                dma((2, levels)), dma((2, levels)),
                dma((2, 2)), dma((2, 2)),
                dma, dma,
                dma((2, half)), dma((2, half)),
                dma, dma,
                dma((2, half)), dma((2, half)),
            ],
            compiler_params=pltpu.CompilerParams(
                collective_id=0, has_side_effects=True, vmem_limit_bytes=56 * 1024 * 1024
            ),
            name="envar",
        )(
            alpha_field[0],
            perturbation[0],
            obs_value.transpose(0, 2, 1),
            obs_mask.transpose(0, 2, 1),
            obs_precision,
            loc_width,
        )
        return gradient[None], increment.transpose(0, 2, 1)

    return jax.shard_map(
        body,
        mesh=mesh,
        in_specs=(
            P("member", "lev", "lat", None),
            P("member", "lev", "lat", None),
            P("lev", "lat", "member"),
            P("lev", "lat", "member"),
            P("lev"),
            P("lev"),
        ),
        out_specs=(P("member", "lev", "lat", None), P("lev", "lat", "member")),
        check_vma=False,
    )
```

```python
import functools
import math

import jax
import jax.numpy as jnp
from jax import lax
from jax.experimental import pallas as pl
from jax.experimental.pallas import tpu as pltpu
from jax.sharding import PartitionSpec as P

HALO = 24
GROUPS = 2
PAIRS = 2
BLOCK = 256
VERT_SCALE = 2.0
F32 = jnp.float32
BF16 = jnp.bfloat16
MESH = pl.DeviceIdType.MESH

SIDE = [(0, 3), (3, 6), (3, 4), (3, 2), (6, 8), (6, 7), (4, 5), (2, 1)]
TREE = SIDE + [(-p, -c) for p, c in SIDE if c < 8]


def tree_depth(node):
    return 0 if node == 0 else 1 + tree_depth(next(p for p, c in TREE if c == node))


def round_up(value, to):
    return -(-value // to) * to


def vert_weight(diff):
    return 0.5 * math.exp(-diff * diff / (2.0 * VERT_SCALE * VERT_SCALE))


def vert_weights(lev, levels):
    near = [[vert_weight(i - j) for j in range(levels)] for i in range(levels)]
    far = [
        [
            jnp.where(lev == 0, jnp.float32(vert_weight(i - j - levels)), jnp.float32(vert_weight(i - j + levels)))
            for j in range(levels)
        ]
        for i in range(levels)
    ]
    return near, far


def mix(near, far, a, b, i):
    value = near[i][0] * a[0]
    for j in range(1, len(a)):
        value = value + near[i][j] * a[j]
    for j in range(len(b)):
        value = value + far[i][j] * b[j]
    return value


def remainder_rows(chunk):
    return round_up(-(-chunk // 4), 8)


def packed_rows(chunk):
    return round_up(chunk + remainder_rows(chunk), 16)


def pack(value):
    chunk = value.shape[0]
    part = remainder_rows(chunk)
    rest = value[:, 128:256]
    tail = rest[0:part]
    for g in range(1, 4):
        piece = rest[g * part : min((g + 1) * part, chunk)]
        if piece.shape[0] == 0:
            continue
        if piece.shape[0] < part:
            piece = jnp.concatenate([piece, jnp.zeros((part - piece.shape[0], 128), value.dtype)], axis=0)
        tail = tail + pltpu.roll(piece, 32 * g, 1)
    parts = [value[:, 0:128], tail]
    left = packed_rows(chunk) - chunk - part
    if left:
        parts.append(jnp.zeros((left, 128), value.dtype))
    return jnp.concatenate(parts, axis=0)


def unpack(value, chunk):
    part = remainder_rows(chunk)
    tail = value[chunk : chunk + part]
    pieces = [tail]
    for g in range(1, 4):
        keep = min(part, chunk - g * part)
        if keep > 0:
            pieces.append(pltpu.roll(tail, 128 - 32 * g, 1)[0:keep])
    return jnp.concatenate([value[0:chunk], jnp.concatenate(pieces, axis=0)], axis=1)


def kernel(
    ring, lat_count, lev_count,
    alpha, pert, obs, mask, prec, width,
    back_out, far_out, inc,
    own, far, band, edge_f, edge, halo, latk, table, rolled, flat, turned,
    terms, sum_tx, sum_rx, pair_tx, pair_rx, site, total, seen, adj, back,
    lev_send, lev_recv, halo_send, halo_recv, site_send, site_recv,
    sum_send, sum_recv, pair_send, pair_recv, gather_send, gather_recv, out_sem,
):
    levels, rows, cols = alpha.shape
    blocks = cols // BLOCK
    cell = cols // (ring * GROUPS)
    chunk_rows = GROUPS * cell
    pad = flat.shape[0]
    deep = levels // PAIRS
    used = deep * rows
    nodes = [0] + [c for _, c in TREE]
    index = {c: i for i, (_, c) in enumerate(TREE)}
    parent = {c: p for p, c in TREE}
    children = {n: [c for p, c in TREE if p == n] for n in nodes}
    depth = {n: tree_depth(n) for n in nodes}
    height = {}
    for n in sorted(nodes, key=lambda n: -depth[n]):
        height[n] = 1 + max([height[c] for c in children[n]], default=-1)

    member = lax.axis_index("member")
    lat = lax.axis_index("lat")
    lev = lax.axis_index("lev")
    z = lax.rem(member, ring)
    group = lax.div(member, ring)

    def place(offset):
        return lax.rem(z + (ring + offset), ring)

    def at(offset):
        return {"member": group * ring + place(offset)}

    pair = {"member": lax.rem(member + ring, ring * GROUPS)}
    south = {"lat": lax.rem(lat + 1, lat_count)}
    north = {"lat": lax.rem(lat + lat_count - 1, lat_count)}
    sibling = {"lev": 1 - lev}

    def remote(src, dst, send, recv, to):
        return pltpu.make_async_remote_copy(
            src_ref=src, dst_ref=dst, send_sem=send, recv_sem=recv, device_id=to, device_id_type=MESH
        )

    def lev_copy(phase, level):
        src, dst = ((own, far), (back, far_out))[phase]
        return remote(src.at[level], dst.at[level], lev_send.at[phase, level], lev_recv.at[phase, level], sibling)

    def halo_copy(phase, h, side):
        return remote(
            edge.at[phase, h, side], halo.at[phase, h, 1 - side],
            halo_send.at[phase, h, side], halo_recv.at[phase, h, 1 - side], (north, south)[side],
        )

    def site_copy(whose):
        return remote(site.at[whose], site.at[whose], site_send, site_recv, pair)

    def sum_copy(h, node):
        i = index[node]
        to = at(parent[node] - node)
        return remote(sum_tx.at[h, i], sum_rx.at[h, i], sum_send.at[h, i], sum_recv.at[h, i], to)

    def pair_copy(h):
        return remote(pair_tx.at[h], pair_rx.at[h], pair_send.at[h], pair_recv.at[h], pair)

    def gather_copy(h, node, holder):
        i = index[node]
        chunk = place(-holder)
        to = at(node - parent[node])
        return remote(adj.at[h, chunk], adj.at[h, chunk], gather_send.at[h, i], gather_recv.at[h, i], to)

    barrier = pltpu.get_barrier_semaphore()
    jumps = sorted({p - c for p, c in TREE} | {c - p for p, c in TREE})
    partners = [sibling, south, north, pair] + [at(jump) for jump in jumps]
    for partner in partners:
        pl.semaphore_signal(barrier, inc=1, device_id=partner, device_id_type=MESH)

    def round_level(level, carry):
        own[level] = alpha[level].astype(BF16)
        return carry

    lax.fori_loop(0, levels, round_level, 0)

    site[group] = jnp.zeros(site.shape[1:], F32)
    for level in range(levels):
        lanes = slice((level % deep) * rows, (level % deep + 1) * rows)
        site[group, level // deep, 0, :, lanes] = obs[level]
        site[group, level // deep, 1, :, lanes] = mask[level].astype(F32) * prec[level]

    def build_latk(level, carry):
        scale = jnp.full((1, 128), width[level].astype(F32), F32) / 3.0
        lane = lax.broadcasted_iota(jnp.int32, (1, 128), 1)
        step = (lane - HALO).astype(F32)
        norm_sq = jnp.sum(
            jnp.where(lane <= 2 * HALO, jnp.exp(-(step * step) / (scale * scale)), 0.0), axis=1, keepdims=True
        )
        row = lax.broadcasted_iota(jnp.int32, (rows, 128), 0)
        col = lax.broadcasted_iota(jnp.int32, (rows, 128), 1)
        is_top = jnp.logical_and(col >= rows, col < rows + HALO)
        is_bottom = col >= rows + HALO
        spot = jnp.where(is_top, col - rows - HALO, col)
        spot = jnp.where(is_bottom, col - HALO, spot)
        diff = spot - row
        keep = jnp.abs(diff) <= HALO
        keep = jnp.logical_and(keep, jnp.logical_or(jnp.logical_not(is_top), lat > 0))
        keep = jnp.logical_and(keep, jnp.logical_or(jnp.logical_not(is_bottom), lat < lat_count - 1))
        dist = diff.astype(F32)
        weight = jnp.exp(-(dist * dist) / (2.0 * scale * scale)) / jnp.sqrt(norm_sq)
        weight = jnp.where(keep, weight, 0.0)
        high = weight.astype(BF16)
        latk[level, 0:rows] = high
        latk[level, rows : 2 * rows] = (weight - high.astype(F32)).astype(BF16)
        return carry

    lax.fori_loop(0, levels, build_latk, 0)

    def build_table(level, carry):
        scale = jnp.full((1, 128), width[level].astype(F32), F32)[:, 0:1]
        square = scale * scale
        spot = lax.broadcasted_iota(jnp.int32, (1, cols), 1)
        cycle = jnp.minimum(spot, cols - spot).astype(F32)
        norm_sq = jnp.sum(jnp.exp(-(cycle * cycle) / square), axis=1, keepdims=True)
        inverse = 1.0 / jnp.sqrt(norm_sq)
        factor = -1.0 / (2.0 * square)
        step = 64

        def some(i, inner):
            row = lax.broadcasted_iota(jnp.int32, (step, BLOCK), 0) + i * step
            col = lax.broadcasted_iota(jnp.int32, (step, BLOCK), 1)
            diff = jnp.abs(row - col)
            dist = jnp.minimum(diff, cols - diff).astype(F32)
            table[level, pl.ds(pl.multiple_of(i * step, step), step)] = (
                jnp.exp(dist * dist * factor) * inverse
            ).astype(BF16)
            return inner

        return lax.fori_loop(0, cols // step, some, carry)

    lax.fori_loop(0, deep, build_table, 0)
    flat[used:pad] = jnp.zeros((pad - used, cols), F32)
    pl.semaphore_wait(barrier, len(partners))

    for level in range(levels):
        lev_copy(0, level).start()
    site_copy(group).start()

    near_weights, far_weights = vert_weights(lev, levels)
    row_chunks = list(range(rows // 16))
    outer = [c for c in row_chunks if 16 * c < HALO or 16 * c + 16 > rows - HALO]
    inner_chunks = [c for c in row_chunks if c not in outer]

    def lane_loop(body):
        def step(block, carry):
            body(pl.ds(pl.multiple_of(block * BLOCK, BLOCK), BLOCK))
            return carry

        lax.fori_loop(0, blocks, step, 0)

    def vertical(outs, chunks):
        def body(lanes):
            for chunk in chunks:
                first = 16 * chunk
                part = slice(first, first + 16)
                a = [own[j, part, lanes].astype(F32) for j in range(levels)]
                b = [far[j, part, lanes].astype(F32) for j in range(levels)]
                for i in outs:
                    value = mix(near_weights, far_weights, a, b, i)
                    band[i, part, lanes] = value.astype(BF16)
                    top = min(HALO, first + 16) - first
                    if top > 0:
                        edge_f[0, HALO * i + first : HALO * i + first + top, lanes] = value[0:top]
                    skip = max(0, rows - HALO - first)
                    if skip < 16:
                        start = HALO * i + first + skip - (rows - HALO)
                        edge_f[1, start : start + 16 - skip, lanes] = value[skip:16]

        lane_loop(body)

    def send_edges(phase, h):
        def body(lanes):
            for side in range(2):
                part = slice(h * deep * HALO, (h + 1) * deep * HALO)
                edge[phase, h, side, :, lanes] = edge_f[side, part, lanes].astype(BF16)

        lane_loop(body)
        for side in range(2):
            halo_copy(phase, h, side).start()

    def receive_edges(phase, h):
        for side in range(2):
            halo_copy(phase, h, side).wait_recv()

        def body(lanes):
            top = halo[phase, h, 0, :, lanes].astype(F32)
            bottom = halo[phase, h, 1, :, lanes].astype(F32)
            for i in range(deep):
                part = slice(HALO * i, HALO * i + HALO)
                band[h * deep + i, rows : rows + 2 * HALO, lanes] = jnp.concatenate(
                    [top[part], bottom[part]], axis=0
                ).astype(BF16)

        lane_loop(body)

    def smooth(level, block):
        both = jnp.dot(latk[level], band[level, :, block * BLOCK : (block + 1) * BLOCK], preferred_element_type=F32)
        return (both[0:rows] + both[rows : 2 * rows]).astype(BF16)

    def spread_out(block, value):
        for turn in range(blocks):
            start = ((block - turn) % blocks) * BLOCK
            rolled[turn * rows : (turn + 1) * rows, start : start + BLOCK] = value

    def along_longitude(level):
        return jnp.dot(rolled[...], table[level], preferred_element_type=F32)

    def split_rows(chunk):
        return [pl.ds(pl.multiple_of(g * (cols // GROUPS) + chunk * cell, 8), cell) for g in range(GROUPS)]

    def forward(h):
        def body(i, carry):
            level = h * deep + i
            for block in range(blocks):
                spread_out(block, smooth(level, block))
            out = along_longitude(level)
            here = pl.ds(pl.multiple_of(i * rows, 16), rows)
            for block in range(blocks):
                lanes = slice(block * BLOCK, (block + 1) * BLOCK)
                flat[here, lanes] = out[block * rows : (block + 1) * rows] * pert[level, :, lanes].astype(F32)
            return carry

        lax.fori_loop(0, deep, body, 0)

        def turn(i, carry):
            part = pl.ds(pl.multiple_of(i * 128, 128), 128)
            turned[part, :] = flat[:, part].T
            return carry

        lax.fori_loop(0, cols // 128, turn, 0)

        def fill(chunk, carry):
            terms[h, chunk] = pack(jnp.concatenate([turned[part, :] for part in split_rows(chunk)], axis=0))
            return carry

        lax.fori_loop(0, ring, fill, 0)

    def sum_at(h, node):
        value = terms[h, place(-node)]
        for child in children[node]:
            sum_copy(h, child).wait_recv()
            value = value + sum_rx[h, index[child]].astype(F32)
        return value

    def sum_level(h, which):
        for node in nodes:
            if node != 0 and height[node] == which:
                sum_tx[h, index[node]] = sum_at(h, node).astype(BF16)
                sum_copy(h, node).start()

    def sum_root(h):
        value = sum_at(h, 0)
        total[h] = value
        pair_tx[h] = value.astype(BF16)
        pair_copy(h).start()

    def see(h):
        for kind in range(2):
            both = jnp.concatenate([site[g, h, kind] for g in range(GROUPS)], axis=0)
            seen[h, kind] = pack(both)

    def start_gather(h, node):
        for child in children[node]:
            gather_copy(h, child, node).start()

    def adjoint(h):
        pair_copy(h).wait_recv()
        summed = total[h] + pair_rx[h].astype(F32)
        adj[h, z] = (seen[h, 1] * (summed - seen[h, 0])).astype(BF16)
        start_gather(h, 0)
        total[h] = summed

    def gather_level(h, which):
        for node in nodes:
            if node != 0 and depth[node] == which:
                gather_copy(h, node, node).wait_recv()
                start_gather(h, node)

    def increments(h):
        value = unpack(total[h], chunk_rows)
        turned[0:chunk_rows, :] = value
        mine = turned[pl.ds(pl.multiple_of(group * cell, 8), cell), :]
        for i in range(deep):
            inc[h * deep + i] = mine[:, i * rows : (i + 1) * rows]

    def backward(h):
        def open_up(chunk, carry):
            value = unpack(adj[h, chunk].astype(F32), chunk_rows)
            for g, part in enumerate(split_rows(chunk)):
                turned[part, :] = value[g * cell : (g + 1) * cell]
            return carry

        lax.fori_loop(0, ring, open_up, 0)

        def turn(i, carry):
            part = pl.ds(pl.multiple_of(i * 128, 128), 128)
            flat[:, part] = turned[part, :].T
            return carry

        lax.fori_loop(0, cols // 128, turn, 0)

        def body(i, carry):
            level = h * deep + i
            here = pl.ds(pl.multiple_of(i * rows, 16), rows)
            for block in range(blocks):
                lanes = slice(block * BLOCK, (block + 1) * BLOCK)
                spread_out(block, (flat[here, lanes] * pert[level, :, lanes].astype(F32)).astype(BF16))
            out = along_longitude(level)
            reach = pl.ds(pl.multiple_of(level * HALO, 8), HALO)
            for block in range(blocks):
                lanes = slice(block * BLOCK, (block + 1) * BLOCK)
                value = out[block * rows : (block + 1) * rows]
                band[level, 0:rows, lanes] = value.astype(BF16)
                edge_f[0, reach, lanes] = value[0:HALO]
                edge_f[1, reach, lanes] = value[rows - HALO : rows]
            return carry

        lax.fori_loop(0, deep, body, 0)

    def out_copy(level):
        return pltpu.make_async_copy(back.at[level], back_out.at[level], out_sem.at[level])

    def finish(h):
        for i in range(deep):
            level = h * deep + i
            for block in range(blocks):
                back[level, :, block * BLOCK : (block + 1) * BLOCK] = smooth(level, block)
            lev_copy(1, level).start()
            out_copy(level).start()

    halves = range(PAIRS)
    groups_of = [range(h * deep, (h + 1) * deep) for h in halves]
    for level in range(levels):
        lev_copy(0, level).wait_recv()
    for h in halves:
        vertical(groups_of[h], outer)
        send_edges(0, h)
    vertical(range(levels), inner_chunks)
    lax.fori_loop(deep, levels, build_table, 0)
    for h in halves:
        receive_edges(0, h)
        forward(h)
        sum_level(h, 0)
    site_copy(1 - group).wait_recv()
    for h in halves:
        see(h)
    for which in range(1, height[0]):
        for h in halves:
            sum_level(h, which)
    for h in halves:
        sum_root(h)
    for h in halves:
        adjoint(h)
    for h in halves:
        increments(h)
    for which in range(1, max(depth.values()) + 1):
        for h in halves:
            gather_level(h, which)
    for h in halves:
        backward(h)
        send_edges(1, h)
    for h in halves:
        receive_edges(1, h)
        finish(h)
    for level in range(levels):
        lev_copy(1, level).wait_recv()

    for level in range(levels):
        out_copy(level).wait()
        for phase in range(2):
            lev_copy(phase, level).wait_send()
    for h in halves:
        for phase in range(2):
            for side in range(2):
                halo_copy(phase, h, side).wait_send()
        pair_copy(h).wait_send()
        for node in nodes[1:]:
            sum_copy(h, node).wait_send()
            gather_copy(h, node, parent[node]).wait_send()
    site_copy(group).wait_send()


def last_kernel(alpha, near, far, inc, grad, inc_out):
    levels = alpha.shape[0]
    near_weights, far_weights = vert_weights(lax.axis_index("lev"), levels)

    def step(block, carry):
        lanes = pl.ds(pl.multiple_of(block * BLOCK, BLOCK), BLOCK)
        a = [near[j, :, lanes].astype(F32) for j in range(levels)]
        b = [far[j, :, lanes].astype(F32) for j in range(levels)]
        for i in range(levels):
            grad[i, :, lanes] = alpha[i, :, lanes] + mix(near_weights, far_weights, a, b, i)
        return carry

    lax.fori_loop(0, alpha.shape[2] // BLOCK, step, 0)

    @pl.when(pl.program_id(0) == 0)
    def _():
        inc_out[...] = inc[...]


def solution(mesh):
    ring = mesh.shape["member"] // GROUPS
    lat_count, lev_count = mesh.shape["lat"], mesh.shape["lev"]

    def body(alpha_field, perturbation, obs_value, obs_mask, obs_precision, loc_width):
        _, levels, rows, cols = alpha_field.shape
        cell = obs_value.shape[2]
        deep = levels // PAIRS
        pad = round_up(deep * rows, 128)
        packed = packed_rows(GROUPS * cell)
        edges = len(TREE)
        vmem = pl.BlockSpec(memory_space=pltpu.VMEM)
        smem = pl.BlockSpec(memory_space=pltpu.SMEM)
        hbm = pl.BlockSpec(memory_space=pl.ANY)
        dma = pltpu.SemaphoreType.DMA
        full = (levels, rows, cols)
        alpha = alpha_field[0]
        near, far, increment = pl.pallas_call(
            functools.partial(kernel, ring, lat_count, lev_count),
            out_shape=(
                jax.ShapeDtypeStruct(full, BF16),
                jax.ShapeDtypeStruct(full, BF16),
                jax.ShapeDtypeStruct((levels, cell, rows), F32),
            ),
            in_specs=[vmem, vmem, vmem, vmem, smem, smem],
            out_specs=(hbm, hbm, vmem),
            scratch_shapes=[
                pltpu.VMEM(full, BF16),
                pltpu.VMEM(full, BF16),
                pltpu.VMEM((levels, rows + 2 * HALO, cols), BF16),
                pltpu.VMEM((2, levels * HALO, cols), F32),
                pltpu.VMEM((2, PAIRS, 2, deep * HALO, cols), BF16),
                pltpu.VMEM((2, PAIRS, 2, deep * HALO, cols), BF16),
                pltpu.VMEM((levels, 2 * rows, rows + 2 * HALO), BF16),
                pltpu.VMEM((levels, cols, BLOCK), BF16),
                pltpu.VMEM((cols // BLOCK * rows, cols), BF16),
                pltpu.VMEM((pad, cols), F32),
                pltpu.VMEM((cols, pad), F32),
                pltpu.VMEM((PAIRS, ring, packed, 128), F32),
                pltpu.VMEM((PAIRS, edges, packed, 128), BF16),
                pltpu.VMEM((PAIRS, edges, packed, 128), BF16),
                pltpu.VMEM((PAIRS, packed, 128), BF16),
                pltpu.VMEM((PAIRS, packed, 128), BF16),
                pltpu.VMEM((GROUPS, PAIRS, 2, cell, pad), F32),
                pltpu.VMEM((PAIRS, packed, 128), F32),
                pltpu.VMEM((PAIRS, 2, packed, 128), F32),
                pltpu.VMEM((PAIRS, ring, packed, 128), BF16),
                pltpu.VMEM(full, BF16),
                dma((2, levels)), dma((2, levels)),
                dma((2, PAIRS, 2)), dma((2, PAIRS, 2)),
                dma, dma,
                dma((PAIRS, edges)), dma((PAIRS, edges)),
                dma((PAIRS,)), dma((PAIRS,)),
                dma((PAIRS, edges)), dma((PAIRS, edges)),
                dma((levels,)),
            ],
            compiler_params=pltpu.CompilerParams(
                collective_id=0, has_side_effects=True, vmem_limit_bytes=56 * 1024 * 1024
            ),
            name="envar",
        )(
            alpha,
            perturbation[0],
            obs_value.transpose(0, 2, 1),
            obs_mask.transpose(0, 2, 1),
            obs_precision,
            loc_width,
        )
        part = pl.BlockSpec((levels, 16, cols), lambda i: (0, i, 0))
        whole = pl.BlockSpec((levels, cell, rows), lambda i: (0, 0, 0))
        gradient, increment = pl.pallas_call(
            last_kernel,
            grid=(rows // 16,),
            out_shape=(
                jax.ShapeDtypeStruct(full, F32),
                jax.ShapeDtypeStruct((levels, cell, rows), F32),
            ),
            in_specs=[part, part, part, whole],
            out_specs=(part, whole),
            compiler_params=pltpu.CompilerParams(vmem_limit_bytes=32 * 1024 * 1024),
            name="vertical",
        )(alpha, near, far, increment)
        return gradient[None], increment.transpose(0, 2, 1)

    return jax.shard_map(
        body,
        mesh=mesh,
        in_specs=(
            P("member", "lev", "lat", None),
            P("member", "lev", "lat", None),
            P("lev", "lat", "member"),
            P("lev", "lat", "member"),
            P("lev"),
            P("lev"),
        ),
        out_specs=(P("member", "lev", "lat", None), P("lev", "lat", "member")),
        check_vma=False,
    )
```

```python
import functools
import math

import jax
import jax.numpy as jnp
from jax import lax
from jax.experimental import pallas as pl
from jax.experimental.pallas import tpu as pltpu
from jax.sharding import PartitionSpec as P

HALO = 24
GROUPS = 2
PAIRS = 2
BLOCK = 256
VERT_SCALE = 2.0
F32 = jnp.float32
BF16 = jnp.bfloat16
MESH = pl.DeviceIdType.MESH

SIDE = [(0, 3), (3, 6), (3, 4), (3, 2), (6, 8), (6, 7), (4, 5), (2, 1)]
TREE = SIDE + [(-p, -c) for p, c in SIDE if c < 8]


class Tree:
    def __init__(self, pairs):
        self.nodes = [0] + [c for _, c in pairs]
        self.index = {c: i for i, (_, c) in enumerate(pairs)}
        self.parent = {c: p for p, c in pairs}
        self.children = {n: [c for p, c in pairs if p == n] for n in self.nodes}
        self.height = {}
        for n in sorted(self.nodes, key=lambda n: -self.depth(n)):
            self.height[n] = 1 + max([self.height[c] for c in self.children[n]], default=-1)

    def depth(self, node):
        return 0 if node == 0 else 1 + self.depth(self.parent[node])


def round_up(value, to):
    return -(-value // to) * to


def vert_weight(diff):
    return 0.5 * math.exp(-diff * diff / (2.0 * VERT_SCALE * VERT_SCALE))


def vert_weights(lev, levels):
    near = [[vert_weight(i - j) for j in range(levels)] for i in range(levels)]
    far = [
        [
            jnp.where(lev == 0, jnp.float32(vert_weight(i - j - levels)), jnp.float32(vert_weight(i - j + levels)))
            for j in range(levels)
        ]
        for i in range(levels)
    ]
    return near, far


def mix(near, far, a, b, i):
    value = near[i][0] * a[0]
    for j in range(1, len(a)):
        value = value + near[i][j] * a[j]
    for j in range(len(b)):
        value = value + far[i][j] * b[j]
    return value


def remainder_rows(chunk):
    return round_up(-(-chunk // 4), 8)


def packed_rows(chunk):
    return round_up(chunk + remainder_rows(chunk), 16)


def pack(value):
    chunk = value.shape[0]
    part = remainder_rows(chunk)
    rest = value[:, 128:256]
    tail = rest[0:part]
    for g in range(1, 4):
        piece = rest[g * part : min((g + 1) * part, chunk)]
        if piece.shape[0] == 0:
            continue
        if piece.shape[0] < part:
            piece = jnp.concatenate([piece, jnp.zeros((part - piece.shape[0], 128), value.dtype)], axis=0)
        tail = tail + pltpu.roll(piece, 32 * g, 1)
    parts = [value[:, 0:128], tail]
    left = packed_rows(chunk) - chunk - part
    if left:
        parts.append(jnp.zeros((left, 128), value.dtype))
    return jnp.concatenate(parts, axis=0)


def unpack(value, chunk):
    part = remainder_rows(chunk)
    tail = value[chunk : chunk + part]
    pieces = [tail]
    for g in range(1, 4):
        keep = min(part, chunk - g * part)
        if keep > 0:
            pieces.append(pltpu.roll(tail, 128 - 32 * g, 1)[0:keep])
    return jnp.concatenate([value[0:chunk], jnp.concatenate(pieces, axis=0)], axis=1)


def kernel(
    ring, lat_count, lev_count,
    alpha_in, pert_in, obs_in, mask_in, prec, width,
    back_out, far_out, inc,
    alpha, pert, obs, mask, own, far, band, edge_f, edge, halo, latk, table, rolled, flat, turned,
    mixed, sum_tx, sum_rx, pair_tx, pair_rx, site, total, seen, adj, back,
    load_sem, lev_send, lev_recv, halo_send, halo_recv, site_send, site_recv,
    sum_send, sum_recv, pair_send, pair_recv, gather_send, gather_recv, out_sem,
):
    levels, rows, cols = alpha.shape
    blocks = cols // BLOCK
    cell = cols // (ring * GROUPS)
    chunk_rows = GROUPS * cell
    pad = flat.shape[0]
    deep = levels // PAIRS
    used = deep * rows
    trees = [Tree([(s * p, s * c) for p, c in TREE]) for s in (1, -1)]

    member = lax.axis_index("member")
    lat = lax.axis_index("lat")
    lev = lax.axis_index("lev")
    z = lax.rem(member, ring)
    group = lax.div(member, ring)

    def place(offset):
        return lax.rem(z + (ring + offset), ring)

    def at(offset):
        return {"member": group * ring + place(offset)}

    pair = {"member": lax.rem(member + ring, ring * GROUPS)}
    south = {"lat": lax.rem(lat + 1, lat_count)}
    north = {"lat": lax.rem(lat + lat_count - 1, lat_count)}
    sibling = {"lev": 1 - lev}

    def remote(src, dst, send, recv, to):
        return pltpu.make_async_remote_copy(
            src_ref=src, dst_ref=dst, send_sem=send, recv_sem=recv, device_id=to, device_id_type=MESH
        )

    def lev_copy(phase, level):
        src, dst = ((own, far), (back, far_out))[phase]
        return remote(src.at[level], dst.at[level], lev_send.at[phase, level], lev_recv.at[phase, level], sibling)

    def halo_copy(phase, h, side):
        return remote(
            edge.at[phase, h, side], halo.at[phase, h, 1 - side],
            halo_send.at[phase, h, side], halo_recv.at[phase, h, 1 - side], (north, south)[side],
        )

    def site_copy(whose):
        return remote(site.at[whose], site.at[whose], site_send, site_recv, pair)

    def sum_copy(h, node):
        i = trees[h].index[node]
        to = at(trees[h].parent[node] - node)
        return remote(sum_tx.at[h, i], sum_rx.at[h, i], sum_send.at[h, i], sum_recv.at[h, i], to)

    def pair_copy(h):
        return remote(pair_tx.at[h], pair_rx.at[h], pair_send.at[h], pair_recv.at[h], pair)

    def gather_copy(h, node, holder):
        i = trees[h].index[node]
        chunk = place(-holder)
        to = at(node - trees[h].parent[node])
        return remote(adj.at[h, chunk], adj.at[h, chunk], gather_send.at[h, i], gather_recv.at[h, i], to)

    barrier = pltpu.get_barrier_semaphore()
    jumps = sorted({p - c for p, c in TREE} | {c - p for p, c in TREE})
    partners = [sibling, south, north, pair] + [at(jump) for jump in jumps]
    for partner in partners:
        pl.semaphore_signal(barrier, inc=1, device_id=partner, device_id_type=MESH)

    def load(i, level=None):
        src, dst = ((pert_in, pert), (obs_in, obs), (mask_in, mask))[i] if level is None else (alpha_in.at[level], alpha.at[level])
        return pltpu.make_async_copy(src, dst, load_sem.at[i])

    for level in range(levels):
        load(3 + level, level).start()
    for i in (1, 2, 0):
        load(i).start()

    def round_level(level, carry):
        own[level] = alpha[level].astype(BF16)
        return carry

    for level in range(levels):
        load(3 + level, level).wait()
    lax.fori_loop(0, levels, round_level, 0)
    load(1).wait()
    load(2).wait()

    site[group] = jnp.zeros(site.shape[1:], F32)
    for level in range(levels):
        lanes = slice((level % deep) * rows, (level % deep + 1) * rows)
        site[group, level // deep, 0, :, lanes] = obs[level]
        site[group, level // deep, 1, :, lanes] = mask[level].astype(F32) * prec[level]

    def build_latk(level, carry):
        scale = jnp.full((1, 128), width[level].astype(F32), F32) / 3.0
        lane = lax.broadcasted_iota(jnp.int32, (1, 128), 1)
        step = (lane - HALO).astype(F32)
        norm_sq = jnp.sum(
            jnp.where(lane <= 2 * HALO, jnp.exp(-(step * step) / (scale * scale)), 0.0), axis=1, keepdims=True
        )
        scale = scale[:, 0:1]
        row = lax.broadcasted_iota(jnp.int32, (rows, BLOCK), 0)
        col = lax.broadcasted_iota(jnp.int32, (rows, BLOCK), 1)
        top = rows + HALO * lax.rem(level, deep)
        bottom = top + HALO * deep
        is_top = jnp.logical_and(col >= top, col < top + HALO)
        is_bottom = jnp.logical_and(col >= bottom, col < bottom + HALO)
        spot = jnp.where(is_top, col - top - HALO, col)
        spot = jnp.where(is_bottom, col - bottom + rows, spot)
        diff = spot - row
        keep = jnp.logical_or(
            col < rows,
            jnp.logical_or(jnp.logical_and(is_top, lat > 0), jnp.logical_and(is_bottom, lat < lat_count - 1)),
        )
        keep = jnp.logical_and(keep, jnp.abs(diff) <= HALO)
        dist = diff.astype(F32)
        weight = jnp.exp(-(dist * dist) / (2.0 * scale * scale)) / jnp.sqrt(norm_sq)
        weight = jnp.where(keep, weight, 0.0)
        high = weight.astype(BF16)
        latk[level, 0:rows] = high
        latk[level, rows : 2 * rows] = (weight - high.astype(F32)).astype(BF16)
        return carry

    lax.fori_loop(0, levels, build_latk, 0)

    def build_table(level, carry):
        scale = jnp.full((1, 128), width[level].astype(F32), F32)[:, 0:1]
        square = scale * scale
        spot = lax.broadcasted_iota(jnp.int32, (1, cols), 1)
        cycle = jnp.minimum(spot, cols - spot).astype(F32)
        norm_sq = jnp.sum(jnp.exp(-(cycle * cycle) / square), axis=1, keepdims=True)
        inverse = 1.0 / jnp.sqrt(norm_sq)
        factor = -1.0 / (2.0 * square)
        step = 64

        def some(i, inner):
            row = lax.broadcasted_iota(jnp.int32, (step, BLOCK), 0) + i * step
            col = lax.broadcasted_iota(jnp.int32, (step, BLOCK), 1)
            diff = jnp.abs(row - col)
            dist = jnp.minimum(diff, cols - diff).astype(F32)
            table[level, pl.ds(pl.multiple_of(i * step, step), step)] = (
                jnp.exp(dist * dist * factor) * inverse
            ).astype(BF16)
            return inner

        return lax.fori_loop(0, cols // step, some, carry)

    flat[used:pad] = jnp.zeros((pad - used, cols), F32)
    pl.semaphore_wait(barrier, len(partners))

    for level in range(levels):
        lev_copy(0, level).start()
    site_copy(group).start()

    near_weights, far_weights = vert_weights(lev, levels)
    row_chunks = list(range(rows // 16))
    outer = [c for c in row_chunks if 16 * c < HALO or 16 * c + 16 > rows - HALO]
    inner_chunks = [c for c in row_chunks if c not in outer]

    def lane_loop(body):
        def step(block, carry):
            body(pl.ds(pl.multiple_of(block * BLOCK, BLOCK), BLOCK))
            return carry

        lax.fori_loop(0, blocks, step, 0)

    def vertical(outs, chunks):
        def body(lanes):
            for chunk in chunks:
                first = 16 * chunk
                part = slice(first, first + 16)
                a = [own[j, part, lanes].astype(F32) for j in range(levels)]
                b = [far[j, part, lanes].astype(F32) for j in range(levels)]
                for i in outs:
                    value = mix(near_weights, far_weights, a, b, i)
                    band[i, part, lanes] = value.astype(BF16)
                    top = min(HALO, first + 16) - first
                    if top > 0:
                        edge_f[0, HALO * i + first : HALO * i + first + top, lanes] = value[0:top]
                    skip = max(0, rows - HALO - first)
                    if skip < 16:
                        start = HALO * i + first + skip - (rows - HALO)
                        edge_f[1, start : start + 16 - skip, lanes] = value[skip:16]

        lane_loop(body)

    def send_edges(phase, h):
        def body(lanes):
            for side in range(2):
                part = slice(h * deep * HALO, (h + 1) * deep * HALO)
                edge[phase, h, side, :, lanes] = edge_f[side, part, lanes].astype(BF16)

        lane_loop(body)
        for side in range(2):
            halo_copy(phase, h, side).start()

    def receive_edges(phase, h):
        for side in range(2):
            halo_copy(phase, h, side).wait_recv()

    def smooth(phase, h, level, block):
        lanes = slice(block * BLOCK, (block + 1) * BLOCK)
        spare = BLOCK - rows - 2 * deep * HALO
        field = jnp.concatenate(
            [band[level, :, lanes], halo[phase, h, 0, :, lanes], halo[phase, h, 1, :, lanes], jnp.zeros((spare, BLOCK), BF16)],
            axis=0,
        )
        both = jnp.dot(latk[level], field, preferred_element_type=F32)
        return (both[0:rows] + both[rows : 2 * rows]).astype(BF16)

    def spread_out(block, value):
        for turn in range(blocks):
            start = ((block - turn) % blocks) * BLOCK
            rolled[turn * rows : (turn + 1) * rows, start : start + BLOCK] = value

    def along_longitude(level):
        return jnp.dot(rolled[...], table[level], preferred_element_type=F32)

    def split_rows(chunk):
        return [pl.ds(pl.multiple_of(g * (cols // GROUPS) + chunk * cell, 8), cell) for g in range(GROUPS)]

    def forward(h):
        def body(i, carry):
            level = h * deep + i
            for block in range(blocks):
                spread_out(block, smooth(0, h, level, block))
            out = along_longitude(level)
            here = pl.ds(pl.multiple_of(i * rows, 16), rows)
            for block in range(blocks):
                lanes = slice(block * BLOCK, (block + 1) * BLOCK)
                flat[here, lanes] = out[block * rows : (block + 1) * rows] * pert[level, :, lanes].astype(F32)
            return carry

        lax.fori_loop(0, deep, body, 0)

        def turn(i, carry):
            part = pl.ds(pl.multiple_of(i * 128, 128), 128)
            turned[h, part, :] = flat[:, part].T
            return carry

        lax.fori_loop(0, cols // 128, turn, 0)

    def sum_at(h, node):
        value = pack(jnp.concatenate([turned[h, part, :] for part in split_rows(place(-node))], axis=0))
        for child in trees[h].children[node]:
            sum_copy(h, child).wait_recv()
            value = value + sum_rx[h, trees[h].index[child]].astype(F32)
        return value

    def sum_level(h, which):
        for node in trees[h].nodes[1:]:
            if trees[h].height[node] == which:
                sum_tx[h, trees[h].index[node]] = sum_at(h, node).astype(BF16)
                sum_copy(h, node).start()

    def sum_root(h):
        value = sum_at(h, 0)
        total[h] = value
        pair_tx[h] = value.astype(BF16)
        pair_copy(h).start()

    def see(h):
        for kind in range(2):
            both = jnp.concatenate([site[g, h, kind] for g in range(GROUPS)], axis=0)
            seen[h, kind] = pack(both)

    def start_gather(h, node):
        for child in trees[h].children[node]:
            gather_copy(h, child, node).start()

    def adjoint(h):
        pair_copy(h).wait_recv()
        summed = total[h] + pair_rx[h].astype(F32)
        adj[h, z] = (seen[h, 1] * (summed - seen[h, 0])).astype(BF16)
        start_gather(h, 0)
        total[h] = summed
        open_up(h, z)

    def open_up(h, chunk):
        value = unpack(adj[h, chunk].astype(F32), chunk_rows)
        for g, part in enumerate(split_rows(chunk)):
            turned[h, part, :] = value[g * cell : (g + 1) * cell]

    def gather_level(h, which):
        here = [n for n in trees[h].nodes if trees[h].depth(n) == which]
        for node in here:
            gather_copy(h, node, node).wait_recv()
            start_gather(h, node)
            if not trees[h].children[node]:
                open_up(h, place(-node))
        for node in here:
            if trees[h].children[node]:
                open_up(h, place(-node))

    def increments(h):
        value = unpack(total[h], chunk_rows)
        mixed[...] = value
        mine = mixed[pl.ds(pl.multiple_of(group * cell, 8), cell), :]
        for i in range(deep):
            inc[h * deep + i] = mine[:, i * rows : (i + 1) * rows]

    def backward(h):
        def turn(i, carry):
            part = pl.ds(pl.multiple_of(i * 128, 128), 128)
            flat[:, part] = turned[h, part, :].T
            return carry

        lax.fori_loop(0, cols // 128, turn, 0)

        def body(i, carry):
            level = h * deep + i
            here = pl.ds(pl.multiple_of(i * rows, 16), rows)
            for block in range(blocks):
                lanes = slice(block * BLOCK, (block + 1) * BLOCK)
                spread_out(block, (flat[here, lanes] * pert[level, :, lanes].astype(F32)).astype(BF16))
            out = along_longitude(level)
            reach = pl.ds(pl.multiple_of(level * HALO, 8), HALO)
            for block in range(blocks):
                lanes = slice(block * BLOCK, (block + 1) * BLOCK)
                value = out[block * rows : (block + 1) * rows]
                band[level, :, lanes] = value.astype(BF16)
                edge_f[0, reach, lanes] = value[0:HALO]
                edge_f[1, reach, lanes] = value[rows - HALO : rows]
            return carry

        lax.fori_loop(0, deep, body, 0)

    def out_copy(level):
        return pltpu.make_async_copy(back.at[level], back_out.at[level], out_sem.at[level])

    def finish(h):
        for i in range(deep):
            level = h * deep + i
            for block in range(blocks):
                back[level, :, block * BLOCK : (block + 1) * BLOCK] = smooth(1, h, level, block)
            lev_copy(1, level).start()
            out_copy(level).start()

    halves = range(PAIRS)
    groups_of = [range(h * deep, (h + 1) * deep) for h in halves]
    for level in range(levels):
        lev_copy(0, level).wait_recv()
    for h in halves:
        vertical(groups_of[h], outer)
        send_edges(0, h)
    vertical(range(levels), inner_chunks)
    lax.fori_loop(0, levels, build_table, 0)
    load(0).wait()
    for h in halves:
        receive_edges(0, h)
        forward(h)
        sum_level(h, 0)
    site_copy(1 - group).wait_recv()
    for h in halves:
        see(h)
    for which in range(1, trees[0].height[0]):
        for h in halves:
            sum_level(h, which)
    for h in halves:
        sum_root(h)
    for h in halves:
        adjoint(h)
    for h in halves:
        increments(h)
    for which in range(1, trees[0].height[0] + 1):
        for h in halves:
            gather_level(h, which)
    for h in halves:
        backward(h)
        send_edges(1, h)
    for h in halves:
        receive_edges(1, h)
        finish(h)
    for level in range(levels):
        lev_copy(1, level).wait_recv()

    for level in range(levels):
        out_copy(level).wait()
        for phase in range(2):
            lev_copy(phase, level).wait_send()
    for h in halves:
        for phase in range(2):
            for side in range(2):
                halo_copy(phase, h, side).wait_send()
        pair_copy(h).wait_send()
        for node in trees[h].nodes[1:]:
            sum_copy(h, node).wait_send()
            gather_copy(h, node, trees[h].parent[node]).wait_send()
    site_copy(group).wait_send()


def last_kernel(alpha, near, far, inc, grad, inc_out):
    levels = alpha.shape[0]
    near_weights, far_weights = vert_weights(lax.axis_index("lev"), levels)

    def step(block, carry):
        lanes = pl.ds(pl.multiple_of(block * BLOCK, BLOCK), BLOCK)
        a = [near[j, :, lanes].astype(F32) for j in range(levels)]
        b = [far[j, :, lanes].astype(F32) for j in range(levels)]
        for i in range(levels):
            grad[i, :, lanes] = alpha[i, :, lanes] + mix(near_weights, far_weights, a, b, i)
        return carry

    lax.fori_loop(0, alpha.shape[2] // BLOCK, step, 0)

    @pl.when(pl.program_id(0) == 0)
    def _():
        inc_out[...] = inc[...]


def solution(mesh):
    ring = mesh.shape["member"] // GROUPS
    lat_count, lev_count = mesh.shape["lat"], mesh.shape["lev"]

    def body(alpha_field, perturbation, obs_value, obs_mask, obs_precision, loc_width):
        _, levels, rows, cols = alpha_field.shape
        cell = obs_value.shape[2]
        deep = levels // PAIRS
        pad = round_up(deep * rows, 128)
        packed = packed_rows(GROUPS * cell)
        edges = len(TREE)
        vmem = pl.BlockSpec(memory_space=pltpu.VMEM)
        smem = pl.BlockSpec(memory_space=pltpu.SMEM)
        hbm = pl.BlockSpec(memory_space=pl.ANY)
        dma = pltpu.SemaphoreType.DMA
        full = (levels, rows, cols)
        alpha = alpha_field[0]
        near, far, increment = pl.pallas_call(
            functools.partial(kernel, ring, lat_count, lev_count),
            out_shape=(
                jax.ShapeDtypeStruct(full, BF16),
                jax.ShapeDtypeStruct(full, BF16),
                jax.ShapeDtypeStruct((levels, cell, rows), F32),
            ),
            in_specs=[hbm, hbm, hbm, hbm, smem, smem],
            out_specs=(hbm, hbm, vmem),
            scratch_shapes=[
                pltpu.VMEM(full, F32),
                pltpu.VMEM(full, BF16),
                pltpu.VMEM((levels, cell, rows), F32),
                pltpu.VMEM((levels, cell, rows), jnp.int32),
                pltpu.VMEM(full, BF16),
                pltpu.VMEM(full, BF16),
                pltpu.VMEM(full, BF16),
                pltpu.VMEM((2, levels * HALO, cols), F32),
                pltpu.VMEM((2, PAIRS, 2, deep * HALO, cols), BF16),
                pltpu.VMEM((2, PAIRS, 2, deep * HALO, cols), BF16),
                pltpu.VMEM((levels, 2 * rows, BLOCK), BF16),
                pltpu.VMEM((levels, cols, BLOCK), BF16),
                pltpu.VMEM((cols // BLOCK * rows, cols), BF16),
                pltpu.VMEM((pad, cols), F32),
                pltpu.VMEM((PAIRS, cols, pad), F32),
                pltpu.VMEM((GROUPS * cell, pad), F32),
                pltpu.VMEM((PAIRS, edges, packed, 128), BF16),
                pltpu.VMEM((PAIRS, edges, packed, 128), BF16),
                pltpu.VMEM((PAIRS, packed, 128), BF16),
                pltpu.VMEM((PAIRS, packed, 128), BF16),
                pltpu.VMEM((GROUPS, PAIRS, 2, cell, pad), F32),
                pltpu.VMEM((PAIRS, packed, 128), F32),
                pltpu.VMEM((PAIRS, 2, packed, 128), F32),
                pltpu.VMEM((PAIRS, ring, packed, 128), BF16),
                pltpu.VMEM(full, BF16),
                dma((3 + levels,)),
                dma((2, levels)), dma((2, levels)),
                dma((2, PAIRS, 2)), dma((2, PAIRS, 2)),
                dma, dma,
                dma((PAIRS, edges)), dma((PAIRS, edges)),
                dma((PAIRS,)), dma((PAIRS,)),
                dma((PAIRS, edges)), dma((PAIRS, edges)),
                dma((levels,)),
            ],
            compiler_params=pltpu.CompilerParams(
                collective_id=0, has_side_effects=True, vmem_limit_bytes=56 * 1024 * 1024
            ),
            name="envar",
        )(
            alpha,
            perturbation[0],
            obs_value.transpose(0, 2, 1),
            obs_mask.transpose(0, 2, 1),
            obs_precision,
            loc_width,
        )
        part = pl.BlockSpec((levels, 16, cols), lambda i: (0, i, 0))
        whole = pl.BlockSpec((levels, cell, rows), lambda i: (0, 0, 0))
        gradient, increment = pl.pallas_call(
            last_kernel,
            grid=(rows // 16,),
            out_shape=(
                jax.ShapeDtypeStruct(full, F32),
                jax.ShapeDtypeStruct((levels, cell, rows), F32),
            ),
            in_specs=[part, part, part, whole],
            out_specs=(part, whole),
            compiler_params=pltpu.CompilerParams(vmem_limit_bytes=60 * 1024 * 1024),
            name="vertical",
        )(alpha, near, far, increment)
        return gradient[None], increment.transpose(0, 2, 1)

    return jax.shard_map(
        body,
        mesh=mesh,
        in_specs=(
            P("member", "lev", "lat", None),
            P("member", "lev", "lat", None),
            P("lev", "lat", "member"),
            P("lev", "lat", "member"),
            P("lev"),
            P("lev"),
        ),
        out_specs=(P("member", "lev", "lat", None), P("lev", "lat", "member")),
        check_vma=False,
    )
```

```python
import functools
import math

import jax
import jax.numpy as jnp
from jax import lax
from jax.experimental import pallas as pl
from jax.experimental.pallas import tpu as pltpu
from jax.sharding import PartitionSpec as P

HALO = 24
GROUPS = 2
PAIRS = 2
BLOCK = 256
VERT_SCALE = 2.0
F32 = jnp.float32
BF16 = jnp.bfloat16
MESH = pl.DeviceIdType.MESH

SIDE = [(0, 3), (3, 6), (3, 4), (3, 2), (6, 8), (6, 7), (4, 5), (2, 1)]
TREE = SIDE + [(-p, -c) for p, c in SIDE if c < 8]


class Tree:
    def __init__(self, pairs):
        self.nodes = [0] + [c for _, c in pairs]
        self.index = {c: i for i, (_, c) in enumerate(pairs)}
        self.parent = {c: p for p, c in pairs}
        self.children = {n: [c for p, c in pairs if p == n] for n in self.nodes}
        self.height = {}
        for n in sorted(self.nodes, key=lambda n: -self.depth(n)):
            self.height[n] = 1 + max([self.height[c] for c in self.children[n]], default=-1)

    def depth(self, node):
        return 0 if node == 0 else 1 + self.depth(self.parent[node])


def round_up(value, to):
    return -(-value // to) * to


def vert_weight(diff):
    return 0.5 * math.exp(-diff * diff / (2.0 * VERT_SCALE * VERT_SCALE))


def vert_weights(lev, levels):
    near = [[vert_weight(i - j) for j in range(levels)] for i in range(levels)]
    far = [
        [
            jnp.where(lev == 0, jnp.float32(vert_weight(i - j - levels)), jnp.float32(vert_weight(i - j + levels)))
            for j in range(levels)
        ]
        for i in range(levels)
    ]
    return near, far


def mix(near, far, a, b, i):
    value = near[i][0] * a[0]
    for j in range(1, len(a)):
        value = value + near[i][j] * a[j]
    for j in range(len(b)):
        value = value + far[i][j] * b[j]
    return value


def remainder_rows(chunk):
    return round_up(-(-chunk // 4), 8)


def packed_rows(chunk):
    return round_up(chunk + remainder_rows(chunk), 16)


def pack(value):
    chunk = value.shape[0]
    part = remainder_rows(chunk)
    rest = value[:, 128:256]
    tail = rest[0:part]
    for g in range(1, 4):
        piece = rest[g * part : min((g + 1) * part, chunk)]
        if piece.shape[0] == 0:
            continue
        if piece.shape[0] < part:
            piece = jnp.concatenate([piece, jnp.zeros((part - piece.shape[0], 128), value.dtype)], axis=0)
        tail = tail + pltpu.roll(piece, 32 * g, 1)
    parts = [value[:, 0:128], tail]
    left = packed_rows(chunk) - chunk - part
    if left:
        parts.append(jnp.zeros((left, 128), value.dtype))
    return jnp.concatenate(parts, axis=0)


def unpack(value, chunk):
    part = remainder_rows(chunk)
    tail = value[chunk : chunk + part]
    pieces = [tail]
    for g in range(1, 4):
        keep = min(part, chunk - g * part)
        if keep > 0:
            pieces.append(pltpu.roll(tail, 128 - 32 * g, 1)[0:keep])
    return jnp.concatenate([value[0:chunk], jnp.concatenate(pieces, axis=0)], axis=1)


def kernel(
    ring, lat_count, lev_count,
    alpha_in, pert_in, obs_in, mask_in, prec_in, width_in,
    back, far_out, inc,
    alpha, pert, obs, mask, prec, width, own, far, band, edge_f, edge, halo, latk, table, rolled, flat, turned,
    mixed, sum_tx, sum_rx, pair_tx, pair_rx, site, total, seen, adj,
    load_sem, lev_send, lev_recv, halo_send, halo_recv, site_send, site_recv,
    sum_send, sum_recv, pair_send, pair_recv, gather_send, gather_recv,
):
    levels, rows, cols = alpha.shape
    blocks = cols // BLOCK
    cell = cols // (ring * GROUPS)
    chunk_rows = GROUPS * cell
    pad = flat.shape[0]
    deep = levels // PAIRS
    used = deep * rows
    trees = [Tree([(s * p, s * c) for p, c in TREE]) for s in (1, -1)]

    member = lax.axis_index("member")
    lat = lax.axis_index("lat")
    lev = lax.axis_index("lev")
    z = lax.rem(member, ring)
    group = lax.div(member, ring)

    def place(offset):
        return lax.rem(z + (ring + offset), ring)

    def at(offset):
        return {"member": group * ring + place(offset)}

    pair = {"member": lax.rem(member + ring, ring * GROUPS)}
    south = {"lat": lax.rem(lat + 1, lat_count)}
    north = {"lat": lax.rem(lat + lat_count - 1, lat_count)}
    sibling = {"lev": 1 - lev}

    def remote(src, dst, send, recv, to):
        return pltpu.make_async_remote_copy(
            src_ref=src, dst_ref=dst, send_sem=send, recv_sem=recv, device_id=to, device_id_type=MESH
        )

    def lev_copy(phase, level):
        src, dst = ((own, far), (back, far_out))[phase]
        return remote(src.at[level], dst.at[level], lev_send.at[phase, level], lev_recv.at[phase, level], sibling)

    def halo_copy(phase, h, side):
        return remote(
            edge.at[phase, h, side], halo.at[phase, h, 1 - side],
            halo_send.at[phase, h, side], halo_recv.at[phase, h, 1 - side], (north, south)[side],
        )

    def site_copy(whose):
        return remote(site.at[whose], site.at[whose], site_send, site_recv, pair)

    def sum_copy(h, node):
        i = trees[h].index[node]
        to = at(trees[h].parent[node] - node)
        return remote(sum_tx.at[h, i], sum_rx.at[h, i], sum_send.at[h, i], sum_recv.at[h, i], to)

    def pair_copy(h):
        return remote(pair_tx.at[h], pair_rx.at[h], pair_send.at[h], pair_recv.at[h], pair)

    def gather_copy(h, node, holder):
        i = trees[h].index[node]
        chunk = place(-holder)
        to = at(node - trees[h].parent[node])
        return remote(adj.at[h, chunk], adj.at[h, chunk], gather_send.at[h, i], gather_recv.at[h, i], to)

    barrier = pltpu.get_barrier_semaphore()
    jumps = sorted({p - c for p, c in TREE} | {c - p for p, c in TREE})
    partners = [sibling, south, north, pair] + [at(jump) for jump in jumps]
    for partner in partners:
        pl.semaphore_signal(barrier, inc=1, device_id=partner, device_id_type=MESH)

    def load(i, level=None):
        if level is None:
            src, dst = ((pert_in, pert), (obs_in, obs), (mask_in, mask), (prec_in, prec), (width_in, width))[i]
        else:
            src, dst = alpha_in.at[level], alpha.at[level]
        return pltpu.make_async_copy(src, dst, load_sem.at[i])

    for level in range(levels):
        load(5 + level, level).start()
    for i in (3, 4, 1, 2, 0):
        load(i).start()

    def round_level(level, carry):
        own[level] = alpha[level].astype(BF16)
        return carry

    for level in range(levels):
        load(5 + level, level).wait()
    lax.fori_loop(0, levels, round_level, 0)
    for i in (3, 4, 1, 2):
        load(i).wait()

    site[group] = jnp.zeros(site.shape[1:], F32)
    for level in range(levels):
        lanes = slice((level % deep) * rows, (level % deep + 1) * rows)
        site[group, level // deep, 0, :, lanes] = obs[level]
        site[group, level // deep, 1, :, lanes] = mask[level].astype(F32) * prec[level]

    def build_latk(level, carry):
        scale = jnp.full((1, 128), width[level].astype(F32), F32) / 3.0
        lane = lax.broadcasted_iota(jnp.int32, (1, 128), 1)
        step = (lane - HALO).astype(F32)
        norm_sq = jnp.sum(
            jnp.where(lane <= 2 * HALO, jnp.exp(-(step * step) / (scale * scale)), 0.0), axis=1, keepdims=True
        )
        scale = scale[:, 0:1]
        row = lax.broadcasted_iota(jnp.int32, (rows, BLOCK), 0)
        col = lax.broadcasted_iota(jnp.int32, (rows, BLOCK), 1)
        top = rows + HALO * lax.rem(level, deep)
        bottom = top + HALO * deep
        is_top = jnp.logical_and(col >= top, col < top + HALO)
        is_bottom = jnp.logical_and(col >= bottom, col < bottom + HALO)
        spot = jnp.where(is_top, col - top - HALO, col)
        spot = jnp.where(is_bottom, col - bottom + rows, spot)
        diff = spot - row
        keep = jnp.logical_or(
            col < rows,
            jnp.logical_or(jnp.logical_and(is_top, lat > 0), jnp.logical_and(is_bottom, lat < lat_count - 1)),
        )
        keep = jnp.logical_and(keep, jnp.abs(diff) <= HALO)
        dist = diff.astype(F32)
        weight = jnp.exp(-(dist * dist) / (2.0 * scale * scale)) / jnp.sqrt(norm_sq)
        weight = jnp.where(keep, weight, 0.0)
        high = weight.astype(BF16)
        latk[level, 0:rows] = high
        latk[level, rows : 2 * rows] = (weight - high.astype(F32)).astype(BF16)
        return carry

    lax.fori_loop(0, levels, build_latk, 0)

    def build_table(level, carry):
        scale = jnp.full((1, 128), width[level].astype(F32), F32)[:, 0:1]
        square = scale * scale
        spot = lax.broadcasted_iota(jnp.int32, (1, cols), 1)
        cycle = jnp.minimum(spot, cols - spot).astype(F32)
        norm_sq = jnp.sum(jnp.exp(-(cycle * cycle) / square), axis=1, keepdims=True)
        inverse = 1.0 / jnp.sqrt(norm_sq)
        factor = -1.0 / (2.0 * square)
        step = 64

        def some(i, inner):
            row = lax.broadcasted_iota(jnp.int32, (step, BLOCK), 0) + i * step
            col = lax.broadcasted_iota(jnp.int32, (step, BLOCK), 1)
            diff = jnp.abs(row - col)
            dist = jnp.minimum(diff, cols - diff).astype(F32)
            table[level, pl.ds(pl.multiple_of(i * step, step), step)] = (
                jnp.exp(dist * dist * factor) * inverse
            ).astype(BF16)
            return inner

        return lax.fori_loop(0, cols // step, some, carry)

    for h in range(PAIRS):
        turned[h, :, 128:pad] = jnp.zeros((cols, pad - 128), F32)
    pl.semaphore_wait(barrier, len(partners))

    for level in range(levels):
        lev_copy(0, level).start()
    site_copy(group).start()

    near_weights, far_weights = vert_weights(lev, levels)
    row_chunks = list(range(rows // 16))
    outer = [c for c in row_chunks if 16 * c < HALO or 16 * c + 16 > rows - HALO]
    inner_chunks = [c for c in row_chunks if c not in outer]

    def lane_loop(body):
        def step(block, carry):
            body(pl.ds(pl.multiple_of(block * BLOCK, BLOCK), BLOCK))
            return carry

        lax.fori_loop(0, blocks, step, 0)

    def vertical(outs, chunks):
        def body(lanes):
            for chunk in chunks:
                first = 16 * chunk
                part = slice(first, first + 16)
                a = [own[j, part, lanes].astype(F32) for j in range(levels)]
                b = [far[j, part, lanes].astype(F32) for j in range(levels)]
                for i in outs:
                    value = mix(near_weights, far_weights, a, b, i)
                    band[i, part, lanes] = value.astype(BF16)
                    top = min(HALO, first + 16) - first
                    if top > 0:
                        edge_f[0, HALO * i + first : HALO * i + first + top, lanes] = value[0:top]
                    skip = max(0, rows - HALO - first)
                    if skip < 16:
                        start = HALO * i + first + skip - (rows - HALO)
                        edge_f[1, start : start + 16 - skip, lanes] = value[skip:16]

        lane_loop(body)

    def send_edges(phase, h):
        def body(lanes):
            for side in range(2):
                part = slice(h * deep * HALO, (h + 1) * deep * HALO)
                edge[phase, h, side, :, lanes] = edge_f[side, part, lanes].astype(BF16)

        lane_loop(body)
        for side in range(2):
            halo_copy(phase, h, side).start()

    def receive_edges(phase, h):
        for side in range(2):
            halo_copy(phase, h, side).wait_recv()

    def smooth(phase, h, level, block):
        lanes = slice(block * BLOCK, (block + 1) * BLOCK)
        spare = BLOCK - rows - 2 * deep * HALO
        field = jnp.concatenate(
            [band[level, :, lanes], halo[phase, h, 0, :, lanes], halo[phase, h, 1, :, lanes], jnp.zeros((spare, BLOCK), BF16)],
            axis=0,
        )
        both = jnp.dot(latk[level], field, preferred_element_type=F32)
        return (both[0:rows] + both[rows : 2 * rows]).astype(BF16)

    def spread_out(block, value):
        for turn in range(blocks):
            start = ((block - turn) % blocks) * BLOCK
            rolled[turn * rows : (turn + 1) * rows, start : start + BLOCK] = value

    def along_longitude(level):
        return jnp.dot(rolled[...], table[level], preferred_element_type=F32)

    def split_rows(chunk):
        return [pl.ds(pl.multiple_of(g * (cols // GROUPS) + chunk * cell, 8), cell) for g in range(GROUPS)]

    def forward(h):
        def body(i, carry):
            level = h * deep + i
            for block in range(blocks):
                spread_out(block, smooth(0, h, level, block))
            out = along_longitude(level)
            here = pl.ds(pl.multiple_of(i * rows, 16), rows)
            for block in range(blocks):
                lanes = slice(block * BLOCK, (block + 1) * BLOCK)
                flat[here, lanes] = out[block * rows : (block + 1) * rows] * pert[level, :, lanes].astype(F32)
            return carry

        lax.fori_loop(0, deep, body, 0)

        def turn(i, carry):
            part = pl.ds(pl.multiple_of(i * 128, 128), 128)
            turned[h, part, 0:128] = flat[0:128, part].T
            turned[h, part, 128:used] = flat[128:used, part].T
            return carry

        lax.fori_loop(0, cols // 128, turn, 0)

    def sum_at(h, node):
        value = pack(jnp.concatenate([turned[h, part, :] for part in split_rows(place(-node))], axis=0))
        for child in trees[h].children[node]:
            sum_copy(h, child).wait_recv()
            value = value + sum_rx[h, trees[h].index[child]].astype(F32)
        return value

    def sum_level(h, which):
        for node in trees[h].nodes[1:]:
            if trees[h].height[node] == which:
                sum_tx[h, trees[h].index[node]] = sum_at(h, node).astype(BF16)
                sum_copy(h, node).start()

    def sum_root(h):
        value = sum_at(h, 0)
        total[h] = value
        pair_tx[h] = value.astype(BF16)
        pair_copy(h).start()

    def see(h):
        for kind in range(2):
            both = jnp.concatenate([site[g, h, kind] for g in range(GROUPS)], axis=0)
            seen[h, kind] = pack(both)

    def start_gather(h, node):
        for child in trees[h].children[node]:
            gather_copy(h, child, node).start()

    def adjoint(h):
        pair_copy(h).wait_recv()
        summed = total[h] + pair_rx[h].astype(F32)
        adj[h, z] = (seen[h, 1] * (summed - seen[h, 0])).astype(BF16)
        start_gather(h, 0)
        total[h] = summed
        open_up(h, z)

    def open_up(h, chunk):
        value = unpack(adj[h, chunk].astype(F32), chunk_rows)
        for g, part in enumerate(split_rows(chunk)):
            turned[h, part, :] = value[g * cell : (g + 1) * cell]

    def gather_level(h, which):
        here = [n for n in trees[h].nodes if trees[h].depth(n) == which]
        for node in here:
            gather_copy(h, node, node).wait_recv()
            start_gather(h, node)
            if not trees[h].children[node]:
                open_up(h, place(-node))
        for node in here:
            if trees[h].children[node]:
                open_up(h, place(-node))

    def increments(h):
        value = unpack(total[h], chunk_rows)
        mixed[...] = value
        mine = mixed[pl.ds(pl.multiple_of(group * cell, 8), cell), :]
        for i in range(deep):
            inc[h * deep + i] = mine[:, i * rows : (i + 1) * rows]

    def backward(h):
        def turn(i, carry):
            part = pl.ds(pl.multiple_of(i * 128, 128), 128)
            flat[0:128, part] = turned[h, part, 0:128].T
            flat[128:used, part] = turned[h, part, 128:used].T
            return carry

        lax.fori_loop(0, cols // 128, turn, 0)

        def body(i, carry):
            level = h * deep + i
            here = pl.ds(pl.multiple_of(i * rows, 16), rows)
            for block in range(blocks):
                lanes = slice(block * BLOCK, (block + 1) * BLOCK)
                spread_out(block, (flat[here, lanes] * pert[level, :, lanes].astype(F32)).astype(BF16))
            out = along_longitude(level)
            reach = pl.ds(pl.multiple_of(level * HALO, 8), HALO)
            for block in range(blocks):
                lanes = slice(block * BLOCK, (block + 1) * BLOCK)
                value = out[block * rows : (block + 1) * rows]
                band[level, :, lanes] = value.astype(BF16)
                edge_f[0, reach, lanes] = value[0:HALO]
                edge_f[1, reach, lanes] = value[rows - HALO : rows]
            return carry

        lax.fori_loop(0, deep, body, 0)

    def finish(h):
        for i in range(deep):
            level = h * deep + i
            for block in range(blocks):
                back[level, :, block * BLOCK : (block + 1) * BLOCK] = smooth(1, h, level, block)
            lev_copy(1, level).start()

    halves = range(PAIRS)
    groups_of = [range(h * deep, (h + 1) * deep) for h in halves]
    for level in range(levels):
        lev_copy(0, level).wait_recv()
    for h in halves:
        vertical(groups_of[h], outer)
        send_edges(0, h)
    vertical(range(levels), inner_chunks)
    lax.fori_loop(0, levels, build_table, 0)
    load(0).wait()
    for h in halves:
        receive_edges(0, h)
        forward(h)
        sum_level(h, 0)
    site_copy(1 - group).wait_recv()
    for h in halves:
        see(h)
    for which in range(1, trees[0].height[0]):
        for h in halves:
            sum_level(h, which)
    for h in halves:
        sum_root(h)
    for h in halves:
        adjoint(h)
    for h in halves:
        increments(h)
    last = trees[0].height[0]
    for which in range(1, last):
        for h in halves:
            gather_level(h, which)
    for h in halves:
        gather_level(h, last)
        backward(h)
        send_edges(1, h)
    for h in halves:
        receive_edges(1, h)
        finish(h)
    for level in range(levels):
        lev_copy(1, level).wait_recv()

    for level in range(levels):
        for phase in range(2):
            lev_copy(phase, level).wait_send()
    for h in halves:
        for phase in range(2):
            for side in range(2):
                halo_copy(phase, h, side).wait_send()
        pair_copy(h).wait_send()
        for node in trees[h].nodes[1:]:
            sum_copy(h, node).wait_send()
            gather_copy(h, node, trees[h].parent[node]).wait_send()
    site_copy(group).wait_send()


def last_kernel(alpha, near, far, inc, grad_out, inc_out, grad, store_sem):
    levels, rows, cols = alpha.shape
    near_weights, far_weights = vert_weights(lax.axis_index("lev"), levels)
    parts = [pl.ds(16 * i, 16) for i in range(rows // 16)]

    def store(i):
        return pltpu.make_async_copy(grad.at[:, parts[i]], grad_out.at[:, parts[i]], store_sem.at[i])

    for i, part in enumerate(parts):
        def step(block, carry):
            lanes = pl.ds(pl.multiple_of(block * BLOCK, BLOCK), BLOCK)
            a = [near[j, part, lanes].astype(F32) for j in range(levels)]
            b = [far[j, part, lanes].astype(F32) for j in range(levels)]
            for level in range(levels):
                grad[level, part, lanes] = alpha[level, part, lanes] + mix(near_weights, far_weights, a, b, level)
            return carry

        lax.fori_loop(0, cols // BLOCK, step, 0)
        store(i).start()
    inc_out[...] = inc[...]
    for i in range(len(parts)):
        store(i).wait()


def solution(mesh):
    ring = mesh.shape["member"] // GROUPS
    lat_count, lev_count = mesh.shape["lat"], mesh.shape["lev"]

    def body(alpha_field, perturbation, obs_value, obs_mask, obs_precision, loc_width):
        _, levels, rows, cols = alpha_field.shape
        cell = obs_value.shape[2]
        deep = levels // PAIRS
        pad = round_up(deep * rows, 128)
        packed = packed_rows(GROUPS * cell)
        edges = len(TREE)
        vmem = pl.BlockSpec(memory_space=pltpu.VMEM)
        hbm = pl.BlockSpec(memory_space=pltpu.HBM)
        dma = pltpu.SemaphoreType.DMA
        full = (levels, rows, cols)
        alpha = alpha_field[0]
        near, far, increment = pl.pallas_call(
            functools.partial(kernel, ring, lat_count, lev_count),
            out_shape=(
                pltpu.VMEM(full, BF16),
                pltpu.VMEM(full, BF16),
                jax.ShapeDtypeStruct((levels, cell, rows), F32),
            ),
            in_specs=[hbm] * 6,
            out_specs=(vmem, vmem, vmem),
            scratch_shapes=[
                pltpu.VMEM(full, F32),
                pltpu.VMEM(full, BF16),
                pltpu.VMEM((levels, cell, rows), F32),
                pltpu.VMEM((levels, cell, rows), jnp.int32),
                pltpu.SMEM((levels,), F32),
                pltpu.SMEM((levels,), jnp.int32),
                pltpu.VMEM(full, BF16),
                pltpu.VMEM(full, BF16),
                pltpu.VMEM(full, BF16),
                pltpu.VMEM((2, levels * HALO, cols), F32),
                pltpu.VMEM((2, PAIRS, 2, deep * HALO, cols), BF16),
                pltpu.VMEM((2, PAIRS, 2, deep * HALO, cols), BF16),
                pltpu.VMEM((levels, 2 * rows, BLOCK), BF16),
                pltpu.VMEM((levels, cols, BLOCK), BF16),
                pltpu.VMEM((cols // BLOCK * rows, cols), BF16),
                pltpu.VMEM((pad, cols), F32),
                pltpu.VMEM((PAIRS, cols, pad), F32),
                pltpu.VMEM((GROUPS * cell, pad), F32),
                pltpu.VMEM((PAIRS, edges, packed, 128), BF16),
                pltpu.VMEM((PAIRS, edges, packed, 128), BF16),
                pltpu.VMEM((PAIRS, packed, 128), BF16),
                pltpu.VMEM((PAIRS, packed, 128), BF16),
                pltpu.VMEM((GROUPS, PAIRS, 2, cell, pad), F32),
                pltpu.VMEM((PAIRS, packed, 128), F32),
                pltpu.VMEM((PAIRS, 2, packed, 128), F32),
                pltpu.VMEM((PAIRS, ring, packed, 128), BF16),
                dma((5 + levels,)),
                dma((2, levels)), dma((2, levels)),
                dma((2, PAIRS, 2)), dma((2, PAIRS, 2)),
                dma, dma,
                dma((PAIRS, edges)), dma((PAIRS, edges)),
                dma((PAIRS,)), dma((PAIRS,)),
                dma((PAIRS, edges)), dma((PAIRS, edges)),
            ],
            compiler_params=pltpu.CompilerParams(
                collective_id=0, has_side_effects=True, vmem_limit_bytes=32 * 1024 * 1024
            ),
            name="envar",
        )(
            *[
                pltpu.with_memory_space_constraint(x, pltpu.HBM)
                for x in (
                    alpha,
                    perturbation[0],
                    obs_value.transpose(0, 2, 1),
                    obs_mask.transpose(0, 2, 1),
                    obs_precision,
                    loc_width,
                )
            ]
        )
        gradient, increment = pl.pallas_call(
            last_kernel,
            out_shape=(
                jax.ShapeDtypeStruct(full, F32),
                jax.ShapeDtypeStruct((levels, cell, rows), F32),
            ),
            in_specs=[vmem, vmem, vmem, vmem],
            out_specs=(hbm, vmem),
            scratch_shapes=[
                pltpu.VMEM(full, F32),
                dma((rows // 16,)),
            ],
            compiler_params=pltpu.CompilerParams(vmem_limit_bytes=16 * 1024 * 1024),
            name="vertical",
        )(alpha, near, far, increment)
        return gradient[None], increment.transpose(0, 2, 1)

    return jax.shard_map(
        body,
        mesh=mesh,
        in_specs=(
            P("member", "lev", "lat", None),
            P("member", "lev", "lat", None),
            P("lev", "lat", "member"),
            P("lev", "lat", "member"),
            P("lev"),
            P("lev"),
        ),
        out_specs=(P("member", "lev", "lat", None), P("lev", "lat", "member")),
        check_vma=False,
    )
```

```python
import functools
import math

import jax
import jax.numpy as jnp
from jax import lax
from jax.experimental import pallas as pl
from jax.experimental.pallas import tpu as pltpu
from jax.sharding import PartitionSpec as P

HALO = 24
GROUPS = 2
PAIRS = 2
BLOCK = 256
VERT_SCALE = 2.0
F32 = jnp.float32
BF16 = jnp.bfloat16
MESH = pl.DeviceIdType.MESH

FIRST = [(0, 3), (0, 1), (3, 6), (3, 4), (1, 2), (6, 8), (6, 7), (4, 5)]
SECOND = [(0, 3), (3, 6), (3, 4), (3, 2), (6, 8), (6, 7), (4, 5), (2, 1)]


def both_sides(side, sign):
    return [(sign * p, sign * c) for p, c in side] + [(-sign * p, -sign * c) for p, c in side if c < 8]


TREES = [both_sides(FIRST, 1), both_sides(SECOND, -1)]


class Tree:
    def __init__(self, pairs):
        self.nodes = [0] + [c for _, c in pairs]
        self.index = {c: i for i, (_, c) in enumerate(pairs)}
        self.parent = {c: p for p, c in pairs}
        self.children = {n: [c for p, c in pairs if p == n] for n in self.nodes}
        self.height = {}
        for n in sorted(self.nodes, key=lambda n: -self.depth(n)):
            self.height[n] = 1 + max([self.height[c] for c in self.children[n]], default=-1)

    def depth(self, node):
        return 0 if node == 0 else 1 + self.depth(self.parent[node])


def round_up(value, to):
    return -(-value // to) * to


def vert_weight(diff):
    return 0.5 * math.exp(-diff * diff / (2.0 * VERT_SCALE * VERT_SCALE))


def vert_weights(lev, levels):
    near = [[vert_weight(i - j) for j in range(levels)] for i in range(levels)]
    far = [
        [
            jnp.where(lev == 0, jnp.float32(vert_weight(i - j - levels)), jnp.float32(vert_weight(i - j + levels)))
            for j in range(levels)
        ]
        for i in range(levels)
    ]
    return near, far


def mix(near, far, a, b, i):
    value = near[i][0] * a[0]
    for j in range(1, len(a)):
        value = value + near[i][j] * a[j]
    for j in range(len(b)):
        value = value + far[i][j] * b[j]
    return value


def remainder_rows(chunk):
    return round_up(-(-chunk // 4), 8)


def packed_rows(chunk):
    return chunk + remainder_rows(chunk)


def pack(value):
    chunk = value.shape[0]
    part = remainder_rows(chunk)
    rest = value[:, 128:256]
    tail = rest[0:part]
    for g in range(1, 4):
        piece = rest[g * part : min((g + 1) * part, chunk)]
        if piece.shape[0] == 0:
            continue
        if piece.shape[0] < part:
            piece = jnp.concatenate([piece, jnp.zeros((part - piece.shape[0], 128), value.dtype)], axis=0)
        tail = tail + pltpu.roll(piece, 32 * g, 1)
    parts = [value[:, 0:128], tail]
    left = packed_rows(chunk) - chunk - part
    if left:
        parts.append(jnp.zeros((left, 128), value.dtype))
    return jnp.concatenate(parts, axis=0)


def unpack(value, chunk):
    part = remainder_rows(chunk)
    tail = value[chunk : chunk + part]
    pieces = [tail]
    for g in range(1, 4):
        keep = min(part, chunk - g * part)
        if keep > 0:
            pieces.append(pltpu.roll(tail, 128 - 32 * g, 1)[0:keep])
    return jnp.concatenate([value[0:chunk], jnp.concatenate(pieces, axis=0)], axis=1)


def kernel(
    ring, lat_count, lev_count,
    alpha_in, pert_in, obs_in, mask_in, prec_in, width_in,
    back, far_out, inc,
    alpha, pert, obs, mask, prec, width, own, far, band, edge_f, edge, halo, latk, table, rolled, flat, turned,
    mixed, sum_tx, sum_rx, pair_tx, pair_rx, site, total, seen, adj,
    load_sem, lev_send, lev_recv, halo_send, halo_recv, site_send, site_recv,
    sum_send, sum_recv, pair_send, pair_recv, gather_send, gather_recv,
):
    levels, rows, cols = alpha.shape
    blocks = cols // BLOCK
    cell = cols // (ring * GROUPS)
    chunk_rows = GROUPS * cell
    pad = flat.shape[0]
    deep = levels // PAIRS
    used = deep * rows
    trees = [Tree(pairs) for pairs in TREES]

    member = lax.axis_index("member")
    lat = lax.axis_index("lat")
    lev = lax.axis_index("lev")
    z = lax.rem(member, ring)
    group = lax.div(member, ring)

    def place(offset):
        return lax.rem(z + (ring + offset), ring)

    def at(offset):
        return {"member": group * ring + place(offset)}

    pair = {"member": lax.rem(member + ring, ring * GROUPS)}
    south = {"lat": lax.rem(lat + 1, lat_count)}
    north = {"lat": lax.rem(lat + lat_count - 1, lat_count)}
    sibling = {"lev": 1 - lev}

    def remote(src, dst, send, recv, to):
        return pltpu.make_async_remote_copy(
            src_ref=src, dst_ref=dst, send_sem=send, recv_sem=recv, device_id=to, device_id_type=MESH
        )

    def lev_copy(phase, level):
        src, dst = ((own, far), (back, far_out))[phase]
        return remote(src.at[level], dst.at[level], lev_send.at[phase, level], lev_recv.at[phase, level], sibling)

    def halo_copy(phase, h, side):
        return remote(
            edge.at[phase, h, side], halo.at[phase, h, 1 - side],
            halo_send.at[phase, h, side], halo_recv.at[phase, h, 1 - side], (north, south)[side],
        )

    def site_copy(whose):
        return remote(site.at[whose], site.at[whose], site_send, site_recv, pair)

    def sum_copy(h, node):
        i = trees[h].index[node]
        to = at(trees[h].parent[node] - node)
        return remote(sum_tx.at[h, i], sum_rx.at[h, i], sum_send.at[h, i], sum_recv.at[h, i], to)

    def pair_copy(h):
        return remote(pair_tx.at[h], pair_rx.at[h], pair_send.at[h], pair_recv.at[h], pair)

    def gather_copy(h, node, holder):
        i = trees[h].index[node]
        chunk = place(-holder)
        to = at(node - trees[h].parent[node])
        return remote(adj.at[h, chunk], adj.at[h, chunk], gather_send.at[h, i], gather_recv.at[h, i], to)

    barrier = pltpu.get_barrier_semaphore()
    jumps = sorted({s * (p - c) for pairs in TREES for p, c in pairs for s in (1, -1)})
    partners = [sibling, south, north, pair] + [at(jump) for jump in jumps]
    for partner in partners:
        pl.semaphore_signal(barrier, inc=1, device_id=partner, device_id_type=MESH)

    def load(i, level=None):
        if level is None:
            src, dst = ((pert_in, pert), (obs_in, obs), (mask_in, mask), (prec_in, prec), (width_in, width))[i]
        else:
            src, dst = alpha_in.at[level], alpha.at[level]
        return pltpu.make_async_copy(src, dst, load_sem.at[i])

    for level in range(levels):
        load(5 + level, level).start()
    for i in (3, 4, 1, 2, 0):
        load(i).start()

    def round_level(level, carry):
        own[level] = alpha[level].astype(BF16)
        return carry

    for level in range(levels):
        load(5 + level, level).wait()
    lax.fori_loop(0, levels, round_level, 0)
    pl.semaphore_wait(barrier, len(partners))

    for level in range(levels):
        lev_copy(0, level).start()

    for i in (3, 4, 1, 2):
        load(i).wait()

    site[group] = jnp.zeros(site.shape[1:], F32)
    for level in range(levels):
        lanes = slice((level % deep) * rows, (level % deep + 1) * rows)
        site[group, level // deep, 0, :, lanes] = obs[level]
        site[group, level // deep, 1, :, lanes] = mask[level].astype(F32) * prec[level]

    site_copy(group).start()

    def build_latk(level, carry):
        scale = jnp.full((1, 128), width[level].astype(F32), F32) / 3.0
        lane = lax.broadcasted_iota(jnp.int32, (1, 128), 1)
        step = (lane - HALO).astype(F32)
        norm_sq = jnp.sum(
            jnp.where(lane <= 2 * HALO, jnp.exp(-(step * step) / (scale * scale)), 0.0), axis=1, keepdims=True
        )
        scale = scale[:, 0:1]
        row = lax.broadcasted_iota(jnp.int32, (rows, BLOCK), 0)
        col = lax.broadcasted_iota(jnp.int32, (rows, BLOCK), 1)
        top = rows + HALO * lax.rem(level, deep)
        bottom = top + HALO * deep
        is_top = jnp.logical_and(col >= top, col < top + HALO)
        is_bottom = jnp.logical_and(col >= bottom, col < bottom + HALO)
        spot = jnp.where(is_top, col - top - HALO, col)
        spot = jnp.where(is_bottom, col - bottom + rows, spot)
        diff = spot - row
        keep = jnp.logical_or(
            col < rows,
            jnp.logical_or(jnp.logical_and(is_top, lat > 0), jnp.logical_and(is_bottom, lat < lat_count - 1)),
        )
        keep = jnp.logical_and(keep, jnp.abs(diff) <= HALO)
        dist = diff.astype(F32)
        weight = jnp.exp(-(dist * dist) / (2.0 * scale * scale)) / jnp.sqrt(norm_sq)
        weight = jnp.where(keep, weight, 0.0)
        high = weight.astype(BF16)
        latk[level, 0:rows] = high
        latk[level, rows : 2 * rows] = (weight - high.astype(F32)).astype(BF16)
        return carry

    lax.fori_loop(0, levels, build_latk, 0)

    def build_table(level, carry):
        scale = jnp.full((1, 128), width[level].astype(F32), F32)[:, 0:1]
        square = scale * scale
        spot = lax.broadcasted_iota(jnp.int32, (1, cols), 1)
        cycle = jnp.minimum(spot, cols - spot).astype(F32)
        norm_sq = jnp.sum(jnp.exp(-(cycle * cycle) / square), axis=1, keepdims=True)
        inverse = 1.0 / jnp.sqrt(norm_sq)
        factor = -1.0 / (2.0 * square)
        step = 64

        def some(i, inner):
            row = lax.broadcasted_iota(jnp.int32, (step, BLOCK), 0) + i * step
            col = lax.broadcasted_iota(jnp.int32, (step, BLOCK), 1)
            diff = jnp.abs(row - col)
            dist = jnp.minimum(diff, cols - diff).astype(F32)
            table[level, pl.ds(pl.multiple_of(i * step, step), step)] = (
                jnp.exp(dist * dist * factor) * inverse
            ).astype(BF16)
            return inner

        return lax.fori_loop(0, cols // step, some, carry)

    for h in range(PAIRS):
        turned[h, :, 128:pad] = jnp.zeros((cols, pad - 128), F32)

    near_weights, far_weights = vert_weights(lev, levels)
    row_chunks = list(range(rows // 16))
    outer = [c for c in row_chunks if 16 * c < HALO or 16 * c + 16 > rows - HALO]
    inner_chunks = [c for c in row_chunks if c not in outer]

    def lane_loop(body):
        def step(block, carry):
            body(pl.ds(pl.multiple_of(block * BLOCK, BLOCK), BLOCK))
            return carry

        lax.fori_loop(0, blocks, step, 0)

    def vertical(outs, chunks):
        def body(lanes):
            for chunk in chunks:
                first = 16 * chunk
                part = slice(first, first + 16)
                a = [own[j, part, lanes].astype(F32) for j in range(levels)]
                b = [far[j, part, lanes].astype(F32) for j in range(levels)]
                for i in outs:
                    value = mix(near_weights, far_weights, a, b, i)
                    band[i, part, lanes] = value.astype(BF16)
                    top = min(HALO, first + 16) - first
                    if top > 0:
                        edge_f[0, HALO * i + first : HALO * i + first + top, lanes] = value[0:top]
                    skip = max(0, rows - HALO - first)
                    if skip < 16:
                        start = HALO * i + first + skip - (rows - HALO)
                        edge_f[1, start : start + 16 - skip, lanes] = value[skip:16]

        lane_loop(body)

    def send_edges(phase, h):
        def body(lanes):
            for side in range(2):
                part = slice(h * deep * HALO, (h + 1) * deep * HALO)
                edge[phase, h, side, :, lanes] = edge_f[side, part, lanes].astype(BF16)

        lane_loop(body)
        for side in range(2):
            halo_copy(phase, h, side).start()

    def receive_edges(phase, h):
        for side in range(2):
            halo_copy(phase, h, side).wait_recv()

    def smooth(phase, h, level, block):
        lanes = slice(block * BLOCK, (block + 1) * BLOCK)
        spare = BLOCK - rows - 2 * deep * HALO
        field = jnp.concatenate(
            [band[level, :, lanes], halo[phase, h, 0, :, lanes], halo[phase, h, 1, :, lanes], jnp.zeros((spare, BLOCK), BF16)],
            axis=0,
        )
        both = jnp.dot(latk[level], field, preferred_element_type=F32)
        return (both[0:rows] + both[rows : 2 * rows]).astype(BF16)

    def spread_out(block, value):
        for turn in range(blocks):
            start = ((block - turn) % blocks) * BLOCK
            rolled[turn * rows : (turn + 1) * rows, start : start + BLOCK] = value

    def along_longitude(level):
        return jnp.dot(rolled[...], table[level], preferred_element_type=F32)

    def split_rows(chunk):
        return [pl.ds(pl.multiple_of(g * (cols // GROUPS) + chunk * cell, 8), cell) for g in range(GROUPS)]

    def forward(h):
        def body(i, carry):
            level = h * deep + i
            for block in range(blocks):
                spread_out(block, smooth(0, h, level, block))
            out = along_longitude(level)
            here = pl.ds(pl.multiple_of(i * rows, 16), rows)
            for block in range(blocks):
                lanes = slice(block * BLOCK, (block + 1) * BLOCK)
                flat[here, lanes] = out[block * rows : (block + 1) * rows] * pert[level, :, lanes].astype(F32)
            return carry

        lax.fori_loop(0, deep, body, 0)

        def turn(i, carry):
            part = pl.ds(pl.multiple_of(i * 128, 128), 128)
            turned[h, part, 0:128] = flat[0:128, part].T
            turned[h, part, 128:used] = flat[128:used, part].T
            return carry

        lax.fori_loop(0, cols // 128, turn, 0)

    def sum_at(h, node):
        value = pack(jnp.concatenate([turned[h, part, :] for part in split_rows(place(-node))], axis=0))
        for child in trees[h].children[node]:
            sum_copy(h, child).wait_recv()
            value = value + sum_rx[h, trees[h].index[child]].astype(F32)
        return value

    def sum_level(h, which):
        for node in trees[h].nodes[1:]:
            if trees[h].height[node] == which:
                sum_tx[h, trees[h].index[node]] = sum_at(h, node).astype(BF16)
                sum_copy(h, node).start()

    def sum_root(h):
        value = sum_at(h, 0)
        total[h] = value
        pair_tx[h] = value.astype(BF16)
        pair_copy(h).start()

    def see(h):
        for kind in range(2):
            both = jnp.concatenate([site[g, h, kind] for g in range(GROUPS)], axis=0)
            seen[h, kind] = pack(both)

    def start_gather(h, node):
        for child in trees[h].children[node]:
            gather_copy(h, child, node).start()

    def adjoint(h):
        pair_copy(h).wait_recv()
        summed = total[h] + pair_rx[h].astype(F32)
        adj[h, z] = (seen[h, 1] * (summed - seen[h, 0])).astype(BF16)
        start_gather(h, 0)
        total[h] = summed
        open_up(h, z)

    def open_up(h, chunk):
        value = unpack(adj[h, chunk].astype(F32), chunk_rows)
        for g, part in enumerate(split_rows(chunk)):
            turned[h, part, :] = value[g * cell : (g + 1) * cell]

    def gather_level(h, which):
        here = [n for n in trees[h].nodes if trees[h].depth(n) == which]
        for node in here:
            gather_copy(h, node, node).wait_recv()
            start_gather(h, node)
            if not trees[h].children[node]:
                open_up(h, place(-node))
        for node in here:
            if trees[h].children[node]:
                open_up(h, place(-node))

    def increments(h):
        value = unpack(total[h], chunk_rows)
        mixed[...] = value
        mine = mixed[pl.ds(pl.multiple_of(group * cell, 8), cell), :]
        for i in range(deep):
            inc[h * deep + i] = mine[:, i * rows : (i + 1) * rows]

    def backward(h):
        def turn(i, carry):
            part = pl.ds(pl.multiple_of(i * 128, 128), 128)
            flat[0:128, part] = turned[h, part, 0:128].T
            flat[128:used, part] = turned[h, part, 128:used].T
            return carry

        lax.fori_loop(0, cols // 128, turn, 0)

        def body(i, carry):
            level = h * deep + i
            here = pl.ds(pl.multiple_of(i * rows, 16), rows)
            for block in range(blocks):
                lanes = slice(block * BLOCK, (block + 1) * BLOCK)
                spread_out(block, (flat[here, lanes] * pert[level, :, lanes].astype(F32)).astype(BF16))
            out = along_longitude(level)
            reach = pl.ds(pl.multiple_of(level * HALO, 8), HALO)
            for block in range(blocks):
                lanes = slice(block * BLOCK, (block + 1) * BLOCK)
                value = out[block * rows : (block + 1) * rows]
                band[level, :, lanes] = value.astype(BF16)
                edge_f[0, reach, lanes] = value[0:HALO]
                edge_f[1, reach, lanes] = value[rows - HALO : rows]
            return carry

        lax.fori_loop(0, deep, body, 0)

    def finish(h):
        for i in range(deep):
            level = h * deep + i
            for block in range(blocks):
                back[level, :, block * BLOCK : (block + 1) * BLOCK] = smooth(1, h, level, block)
            lev_copy(1, level).start()

    halves = range(PAIRS)
    groups_of = [range(h * deep, (h + 1) * deep) for h in halves]
    for level in range(levels):
        lev_copy(0, level).wait_recv()
    for h in halves:
        vertical(groups_of[h], outer)
        send_edges(0, h)
    vertical(range(levels), inner_chunks)
    lax.fori_loop(0, levels, build_table, 0)
    load(0).wait()
    for h in halves:
        receive_edges(0, h)
        forward(h)
        sum_level(h, 0)
    site_copy(1 - group).wait_recv()
    for h in halves:
        see(h)
    for which in range(1, max(tree.height[0] for tree in trees)):
        for h in halves:
            sum_level(h, which)
    for h in halves:
        sum_root(h)
    for h in halves:
        adjoint(h)
    for h in halves:
        increments(h)
    lasts = [tree.height[0] for tree in trees]
    for which in range(1, max(lasts)):
        for h in halves:
            if which < lasts[h]:
                gather_level(h, which)
    for h in halves:
        gather_level(h, lasts[h])
        backward(h)
        send_edges(1, h)
    for h in halves:
        receive_edges(1, h)
        finish(h)
    for level in range(levels):
        lev_copy(1, level).wait_recv()

    for level in range(levels):
        for phase in range(2):
            lev_copy(phase, level).wait_send()
    for h in halves:
        for phase in range(2):
            for side in range(2):
                halo_copy(phase, h, side).wait_send()
        pair_copy(h).wait_send()
        for node in trees[h].nodes[1:]:
            sum_copy(h, node).wait_send()
            gather_copy(h, node, trees[h].parent[node]).wait_send()
    site_copy(group).wait_send()


def last_kernel(alpha, near, far, inc, grad_out, inc_out, grad, store_sem):
    levels, rows, cols = alpha.shape
    near_weights, far_weights = vert_weights(lax.axis_index("lev"), levels)
    parts = [pl.ds(16 * i, 16) for i in range(rows // 16)]

    def store(i):
        return pltpu.make_async_copy(grad.at[:, parts[i]], grad_out.at[:, parts[i]], store_sem.at[i])

    for i, part in enumerate(parts):
        def step(block, carry):
            lanes = pl.ds(pl.multiple_of(block * BLOCK, BLOCK), BLOCK)
            a = [near[j, part, lanes].astype(F32) for j in range(levels)]
            b = [far[j, part, lanes].astype(F32) for j in range(levels)]
            for level in range(levels):
                grad[level, part, lanes] = alpha[level, part, lanes] + mix(near_weights, far_weights, a, b, level)
            return carry

        lax.fori_loop(0, cols // BLOCK, step, 0)
        store(i).start()
    inc_out[...] = inc[...]
    for i in range(len(parts)):
        store(i).wait()


def solution(mesh):
    ring = mesh.shape["member"] // GROUPS
    lat_count, lev_count = mesh.shape["lat"], mesh.shape["lev"]

    def body(alpha_field, perturbation, obs_value, obs_mask, obs_precision, loc_width):
        _, levels, rows, cols = alpha_field.shape
        cell = obs_value.shape[2]
        deep = levels // PAIRS
        pad = round_up(deep * rows, 128)
        packed = packed_rows(GROUPS * cell)
        edges = len(TREES[0])
        vmem = pl.BlockSpec(memory_space=pltpu.VMEM)
        hbm = pl.BlockSpec(memory_space=pltpu.HBM)
        dma = pltpu.SemaphoreType.DMA
        full = (levels, rows, cols)
        alpha = alpha_field[0]
        near, far, increment = pl.pallas_call(
            functools.partial(kernel, ring, lat_count, lev_count),
            out_shape=(
                pltpu.VMEM(full, BF16),
                pltpu.VMEM(full, BF16),
                jax.ShapeDtypeStruct((levels, cell, rows), F32),
            ),
            in_specs=[hbm] * 6,
            out_specs=(vmem, vmem, vmem),
            scratch_shapes=[
                pltpu.VMEM(full, F32),
                pltpu.VMEM(full, BF16),
                pltpu.VMEM((levels, cell, rows), F32),
                pltpu.VMEM((levels, cell, rows), jnp.int32),
                pltpu.SMEM((levels,), F32),
                pltpu.SMEM((levels,), jnp.int32),
                pltpu.VMEM(full, BF16),
                pltpu.VMEM(full, BF16),
                pltpu.VMEM(full, BF16),
                pltpu.VMEM((2, levels * HALO, cols), F32),
                pltpu.VMEM((2, PAIRS, 2, deep * HALO, cols), BF16),
                pltpu.VMEM((2, PAIRS, 2, deep * HALO, cols), BF16),
                pltpu.VMEM((levels, 2 * rows, BLOCK), BF16),
                pltpu.VMEM((levels, cols, BLOCK), BF16),
                pltpu.VMEM((cols // BLOCK * rows, cols), BF16),
                pltpu.VMEM((pad, cols), F32),
                pltpu.VMEM((PAIRS, cols, pad), F32),
                pltpu.VMEM((GROUPS * cell, pad), F32),
                pltpu.VMEM((PAIRS, edges, packed, 128), BF16),
                pltpu.VMEM((PAIRS, edges, packed, 128), BF16),
                pltpu.VMEM((PAIRS, packed, 128), BF16),
                pltpu.VMEM((PAIRS, packed, 128), BF16),
                pltpu.VMEM((GROUPS, PAIRS, 2, cell, pad), F32),
                pltpu.VMEM((PAIRS, packed, 128), F32),
                pltpu.VMEM((PAIRS, 2, packed, 128), F32),
                pltpu.VMEM((PAIRS, ring, packed, 128), BF16),
                dma((5 + levels,)),
                dma((2, levels)), dma((2, levels)),
                dma((2, PAIRS, 2)), dma((2, PAIRS, 2)),
                dma, dma,
                dma((PAIRS, edges)), dma((PAIRS, edges)),
                dma((PAIRS,)), dma((PAIRS,)),
                dma((PAIRS, edges)), dma((PAIRS, edges)),
            ],
            compiler_params=pltpu.CompilerParams(
                collective_id=0, has_side_effects=True, vmem_limit_bytes=32 * 1024 * 1024
            ),
            name="envar",
        )(
            *[
                pltpu.with_memory_space_constraint(x, pltpu.HBM)
                for x in (
                    alpha,
                    perturbation[0],
                    obs_value.transpose(0, 2, 1),
                    obs_mask.transpose(0, 2, 1),
                    obs_precision,
                    loc_width,
                )
            ]
        )
        gradient, increment = pl.pallas_call(
            last_kernel,
            out_shape=(
                jax.ShapeDtypeStruct(full, F32),
                jax.ShapeDtypeStruct((levels, cell, rows), F32),
            ),
            in_specs=[vmem, vmem, vmem, vmem],
            out_specs=(hbm, vmem),
            scratch_shapes=[
                pltpu.VMEM(full, F32),
                dma((rows // 16,)),
            ],
            compiler_params=pltpu.CompilerParams(vmem_limit_bytes=16 * 1024 * 1024),
            name="vertical",
        )(alpha, near, far, increment)
        return gradient[None], increment.transpose(0, 2, 1)

    return jax.shard_map(
        body,
        mesh=mesh,
        in_specs=(
            P("member", "lev", "lat", None),
            P("member", "lev", "lat", None),
            P("lev", "lat", "member"),
            P("lev", "lat", "member"),
            P("lev"),
            P("lev"),
        ),
        out_specs=(P("member", "lev", "lat", None), P("lev", "lat", "member")),
        check_vma=False,
    )
```

```python
import functools
import math

import jax
import jax.numpy as jnp
from jax import lax
from jax.experimental import pallas as pl
from jax.experimental.pallas import tpu as pltpu
from jax.sharding import PartitionSpec as P

HALO = 24
GROUPS = 2
PAIRS = 2
BLOCK = 256
VERT_SCALE = 2.0
F32 = jnp.float32
BF16 = jnp.bfloat16
MESH = pl.DeviceIdType.MESH

FIRST = [(0, 3), (0, 1), (3, 6), (3, 4), (1, 2), (6, 8), (6, 7), (4, 5)]
SECOND = [(0, 3), (3, 6), (3, 4), (3, 2), (6, 8), (6, 7), (4, 5), (2, 1)]


def both_sides(side, sign):
    return [(sign * p, sign * c) for p, c in side] + [(-sign * p, -sign * c) for p, c in side if c < 8]


TREES = [both_sides(FIRST, 1), both_sides(SECOND, -1)]


class Tree:
    def __init__(self, pairs):
        self.nodes = [0] + [c for _, c in pairs]
        self.index = {c: i for i, (_, c) in enumerate(pairs)}
        self.parent = {c: p for p, c in pairs}
        self.children = {n: [c for p, c in pairs if p == n] for n in self.nodes}
        self.height = {}
        for n in sorted(self.nodes, key=lambda n: -self.depth(n)):
            self.height[n] = 1 + max([self.height[c] for c in self.children[n]], default=-1)

    def depth(self, node):
        return 0 if node == 0 else 1 + self.depth(self.parent[node])


def round_up(value, to):
    return -(-value // to) * to


def vert_weight(diff):
    return 0.5 * math.exp(-diff * diff / (2.0 * VERT_SCALE * VERT_SCALE))


def vert_weights(lev, levels):
    near = [[vert_weight(i - j) for j in range(levels)] for i in range(levels)]
    far = [
        [
            jnp.where(lev == 0, jnp.float32(vert_weight(i - j - levels)), jnp.float32(vert_weight(i - j + levels)))
            for j in range(levels)
        ]
        for i in range(levels)
    ]
    return near, far


def mix(near, far, a, b, i):
    value = near[i][0] * a[0]
    for j in range(1, len(a)):
        value = value + near[i][j] * a[j]
    for j in range(len(b)):
        value = value + far[i][j] * b[j]
    return value


def remainder_rows(chunk):
    return round_up(-(-chunk // 4), 8)


def packed_rows(chunk):
    return chunk + remainder_rows(chunk)


def pack(value):
    chunk = value.shape[0]
    part = remainder_rows(chunk)
    rest = value[:, 128:256]
    tail = rest[0:part]
    for g in range(1, 4):
        piece = rest[g * part : min((g + 1) * part, chunk)]
        if piece.shape[0] == 0:
            continue
        if piece.shape[0] < part:
            piece = jnp.concatenate([piece, jnp.zeros((part - piece.shape[0], 128), value.dtype)], axis=0)
        tail = tail + pltpu.roll(piece, 32 * g, 1)
    parts = [value[:, 0:128], tail]
    left = packed_rows(chunk) - chunk - part
    if left:
        parts.append(jnp.zeros((left, 128), value.dtype))
    return jnp.concatenate(parts, axis=0)


def unpack(value, chunk):
    part = remainder_rows(chunk)
    tail = value[chunk : chunk + part]
    pieces = [tail]
    for g in range(1, 4):
        keep = min(part, chunk - g * part)
        if keep > 0:
            pieces.append(pltpu.roll(tail, 128 - 32 * g, 1)[0:keep])
    return jnp.concatenate([value[0:chunk], jnp.concatenate(pieces, axis=0)], axis=1)


def kernel(
    ring, lat_count, lev_count,
    alpha_in, pert_in, obs_in, mask_in, prec_in, width_in,
    back, far_out, inc_out,
    alpha, pert, obs, mask, prec, width, own, far, band, edge_f, edge, halo, latk, table, rolled, flat, turned,
    mixed, sum_tx, sum_rx, pair_tx, pair_rx, site, total, seen, adj, inc,
    load_sem, lev_send, lev_recv, halo_send, halo_recv, site_send, site_recv,
    sum_send, sum_recv, pair_send, pair_recv, gather_send, gather_recv, inc_sem,
):
    levels, rows, cols = alpha.shape
    blocks = cols // BLOCK
    cell = cols // (ring * GROUPS)
    chunk_rows = GROUPS * cell
    pad = flat.shape[0]
    deep = levels // PAIRS
    used = deep * rows
    trees = [Tree(pairs) for pairs in TREES]

    member = lax.axis_index("member")
    lat = lax.axis_index("lat")
    lev = lax.axis_index("lev")
    z = lax.rem(member, ring)
    group = lax.div(member, ring)

    def place(offset):
        return lax.rem(z + (ring + offset), ring)

    def at(offset):
        return {"member": group * ring + place(offset)}

    pair = {"member": lax.rem(member + ring, ring * GROUPS)}
    south = {"lat": lax.rem(lat + 1, lat_count)}
    north = {"lat": lax.rem(lat + lat_count - 1, lat_count)}
    sibling = {"lev": 1 - lev}

    def remote(src, dst, send, recv, to):
        return pltpu.make_async_remote_copy(
            src_ref=src, dst_ref=dst, send_sem=send, recv_sem=recv, device_id=to, device_id_type=MESH
        )

    def lev_copy(phase, level):
        src, dst = ((own, far), (back, far_out))[phase]
        return remote(src.at[level], dst.at[level], lev_send.at[phase, level], lev_recv.at[phase, level], sibling)

    def halo_copy(phase, h, side):
        return remote(
            edge.at[phase, h, side], halo.at[phase, h, 1 - side],
            halo_send.at[phase, h, side], halo_recv.at[phase, h, 1 - side], (north, south)[side],
        )

    def site_copy(whose):
        return remote(site.at[whose], site.at[whose], site_send, site_recv, pair)

    def sum_copy(h, node):
        i = trees[h].index[node]
        to = at(trees[h].parent[node] - node)
        return remote(sum_tx.at[h, i], sum_rx.at[h, i], sum_send.at[h, i], sum_recv.at[h, i], to)

    def pair_copy(h):
        return remote(pair_tx.at[h], pair_rx.at[h], pair_send.at[h], pair_recv.at[h], pair)

    def gather_copy(h, node, holder):
        i = trees[h].index[node]
        chunk = place(-holder)
        to = at(node - trees[h].parent[node])
        return remote(adj.at[h, chunk], adj.at[h, chunk], gather_send.at[h, i], gather_recv.at[h, i], to)

    barrier = pltpu.get_barrier_semaphore()
    jumps = sorted({s * (p - c) for pairs in TREES for p, c in pairs for s in (1, -1)})
    partners = [sibling, south, north, pair] + [at(jump) for jump in jumps]
    for partner in partners:
        pl.semaphore_signal(barrier, inc=1, device_id=partner, device_id_type=MESH)

    def load(i, level=None):
        if level is None:
            src, dst = ((pert_in, pert), (obs_in, obs), (mask_in, mask), (prec_in, prec), (width_in, width))[i]
        else:
            src, dst = alpha_in.at[level], alpha.at[level]
        return pltpu.make_async_copy(src, dst, load_sem.at[i])

    for level in range(levels):
        load(5 + level, level).start()
    for i in (3, 4, 1, 2, 0):
        load(i).start()

    def round_level(level, carry):
        own[level] = alpha[level].astype(BF16)
        return carry

    for level in range(levels):
        load(5 + level, level).wait()
    lax.fori_loop(0, levels, round_level, 0)
    pl.semaphore_wait(barrier, len(partners))

    for level in range(levels):
        lev_copy(0, level).start()

    for i in (3, 4, 1, 2):
        load(i).wait()

    site[group] = jnp.zeros(site.shape[1:], F32)
    for level in range(levels):
        lanes = slice((level % deep) * rows, (level % deep + 1) * rows)
        site[group, level // deep, 0, :, lanes] = obs[level]
        site[group, level // deep, 1, :, lanes] = mask[level].astype(F32) * prec[level]

    site_copy(group).start()

    def build_latk(level, carry):
        scale = jnp.full((1, 128), width[level].astype(F32), F32) / 3.0
        lane = lax.broadcasted_iota(jnp.int32, (1, 128), 1)
        step = (lane - HALO).astype(F32)
        norm_sq = jnp.sum(
            jnp.where(lane <= 2 * HALO, jnp.exp(-(step * step) / (scale * scale)), 0.0), axis=1, keepdims=True
        )
        scale = scale[:, 0:1]
        row = lax.broadcasted_iota(jnp.int32, (rows, BLOCK), 0)
        col = lax.broadcasted_iota(jnp.int32, (rows, BLOCK), 1)
        top = rows + HALO * lax.rem(level, deep)
        bottom = top + HALO * deep
        is_top = jnp.logical_and(col >= top, col < top + HALO)
        is_bottom = jnp.logical_and(col >= bottom, col < bottom + HALO)
        spot = jnp.where(is_top, col - top - HALO, col)
        spot = jnp.where(is_bottom, col - bottom + rows, spot)
        diff = spot - row
        keep = jnp.logical_or(
            col < rows,
            jnp.logical_or(jnp.logical_and(is_top, lat > 0), jnp.logical_and(is_bottom, lat < lat_count - 1)),
        )
        keep = jnp.logical_and(keep, jnp.abs(diff) <= HALO)
        dist = diff.astype(F32)
        weight = jnp.exp(-(dist * dist) / (2.0 * scale * scale)) / jnp.sqrt(norm_sq)
        weight = jnp.where(keep, weight, 0.0)
        high = weight.astype(BF16)
        latk[level, 0:rows] = high
        latk[level, rows : 2 * rows] = (weight - high.astype(F32)).astype(BF16)
        return carry

    lax.fori_loop(0, levels, build_latk, 0)

    def build_table(level, carry):
        scale = jnp.full((1, 128), width[level].astype(F32), F32)[:, 0:1]
        square = scale * scale
        spot = lax.broadcasted_iota(jnp.int32, (1, cols), 1)
        cycle = jnp.minimum(spot, cols - spot).astype(F32)
        norm_sq = jnp.sum(jnp.exp(-(cycle * cycle) / square), axis=1, keepdims=True)
        inverse = 1.0 / jnp.sqrt(norm_sq)
        factor = -1.0 / (2.0 * square)
        step = 64

        def some(i, inner):
            row = lax.broadcasted_iota(jnp.int32, (step, BLOCK), 0) + i * step
            col = lax.broadcasted_iota(jnp.int32, (step, BLOCK), 1)
            diff = jnp.abs(row - col)
            dist = jnp.minimum(diff, cols - diff).astype(F32)
            table[level, pl.ds(pl.multiple_of(i * step, step), step)] = (
                jnp.exp(dist * dist * factor) * inverse
            ).astype(BF16)
            return inner

        return lax.fori_loop(0, cols // step, some, carry)

    for h in range(PAIRS):
        turned[h, :, 128:pad] = jnp.zeros((cols, pad - 128), F32)

    near_weights, far_weights = vert_weights(lev, levels)
    row_chunks = list(range(rows // 16))
    outer = [c for c in row_chunks if 16 * c < HALO or 16 * c + 16 > rows - HALO]
    inner_chunks = [c for c in row_chunks if c not in outer]

    def lane_loop(body):
        def step(block, carry):
            body(pl.ds(pl.multiple_of(block * BLOCK, BLOCK), BLOCK))
            return carry

        lax.fori_loop(0, blocks, step, 0)

    def vertical(outs, chunks):
        def body(lanes):
            for chunk in chunks:
                first = 16 * chunk
                part = slice(first, first + 16)
                a = [own[j, part, lanes].astype(F32) for j in range(levels)]
                b = [far[j, part, lanes].astype(F32) for j in range(levels)]
                for i in outs:
                    value = mix(near_weights, far_weights, a, b, i)
                    band[i, part, lanes] = value.astype(BF16)
                    top = min(HALO, first + 16) - first
                    if top > 0:
                        edge_f[0, HALO * i + first : HALO * i + first + top, lanes] = value[0:top]
                    skip = max(0, rows - HALO - first)
                    if skip < 16:
                        start = HALO * i + first + skip - (rows - HALO)
                        edge_f[1, start : start + 16 - skip, lanes] = value[skip:16]

        lane_loop(body)

    def send_edges(phase, h):
        def body(lanes):
            for side in range(2):
                part = slice(h * deep * HALO, (h + 1) * deep * HALO)
                edge[phase, h, side, :, lanes] = edge_f[side, part, lanes].astype(BF16)

        lane_loop(body)
        for side in range(2):
            halo_copy(phase, h, side).start()

    def receive_edges(phase, h):
        for side in range(2):
            halo_copy(phase, h, side).wait_recv()

    def smooth(phase, h, level, block):
        lanes = slice(block * BLOCK, (block + 1) * BLOCK)
        spare = BLOCK - rows - 2 * deep * HALO
        field = jnp.concatenate(
            [band[level, :, lanes], halo[phase, h, 0, :, lanes], halo[phase, h, 1, :, lanes], jnp.zeros((spare, BLOCK), BF16)],
            axis=0,
        )
        both = jnp.dot(latk[level], field, preferred_element_type=F32)
        return (both[0:rows] + both[rows : 2 * rows]).astype(BF16)

    def spread_out(block, value):
        for turn in range(blocks):
            start = ((block - turn) % blocks) * BLOCK
            rolled[turn * rows : (turn + 1) * rows, start : start + BLOCK] = value

    def along_longitude(level):
        return jnp.dot(rolled[...], table[level], preferred_element_type=F32)

    def split_rows(chunk):
        return [pl.ds(pl.multiple_of(g * (cols // GROUPS) + chunk * cell, 8), cell) for g in range(GROUPS)]

    def forward(h):
        def body(i, carry):
            level = h * deep + i
            for block in range(blocks):
                spread_out(block, smooth(0, h, level, block))
            out = along_longitude(level)
            here = pl.ds(pl.multiple_of(i * rows, 16), rows)
            for block in range(blocks):
                lanes = slice(block * BLOCK, (block + 1) * BLOCK)
                flat[here, lanes] = out[block * rows : (block + 1) * rows] * pert[level, :, lanes].astype(F32)
            return carry

        lax.fori_loop(0, deep, body, 0)

        def turn(i, carry):
            part = pl.ds(pl.multiple_of(i * 128, 128), 128)
            turned[h, part, 0:128] = flat[0:128, part].T
            turned[h, part, 128:used] = flat[128:used, part].T
            return carry

        lax.fori_loop(0, cols // 128, turn, 0)

    def sum_at(h, node):
        value = pack(jnp.concatenate([turned[h, part, :] for part in split_rows(place(-node))], axis=0))
        for child in trees[h].children[node]:
            sum_copy(h, child).wait_recv()
            value = value + sum_rx[h, trees[h].index[child]].astype(F32)
        return value

    def sum_level(h, which):
        for node in trees[h].nodes[1:]:
            if trees[h].height[node] == which:
                sum_tx[h, trees[h].index[node]] = sum_at(h, node).astype(BF16)
                sum_copy(h, node).start()

    def sum_root(h):
        value = sum_at(h, 0)
        total[h] = value
        pair_tx[h] = value.astype(BF16)
        pair_copy(h).start()

    def see(h):
        for kind in range(2):
            both = jnp.concatenate([site[g, h, kind] for g in range(GROUPS)], axis=0)
            seen[h, kind] = pack(both)

    def start_gather(h, node):
        for child in trees[h].children[node]:
            gather_copy(h, child, node).start()

    def adjoint(h):
        pair_copy(h).wait_recv()
        summed = total[h] + pair_rx[h].astype(F32)
        adj[h, z] = (seen[h, 1] * (summed - seen[h, 0])).astype(BF16)
        start_gather(h, 0)
        total[h] = summed
        open_up(h, z)

    def open_up(h, chunk):
        value = unpack(adj[h, chunk].astype(F32), chunk_rows)
        for g, part in enumerate(split_rows(chunk)):
            turned[h, part, :] = value[g * cell : (g + 1) * cell]

    def gather_level(h, which):
        here = [n for n in trees[h].nodes if trees[h].depth(n) == which]
        for node in here:
            gather_copy(h, node, node).wait_recv()
            start_gather(h, node)
            if not trees[h].children[node]:
                open_up(h, place(-node))
        for node in here:
            if trees[h].children[node]:
                open_up(h, place(-node))

    def increments(h):
        value = unpack(total[h], chunk_rows)
        mixed[...] = value
        mine = mixed[pl.ds(pl.multiple_of(group * cell, 8), cell), :]
        for i in range(deep):
            inc[h * deep + i] = mine[:, i * rows : (i + 1) * rows]

    def backward(h):
        def turn(i, carry):
            part = pl.ds(pl.multiple_of(i * 128, 128), 128)
            flat[0:128, part] = turned[h, part, 0:128].T
            flat[128:used, part] = turned[h, part, 128:used].T
            return carry

        lax.fori_loop(0, cols // 128, turn, 0)

        def body(i, carry):
            level = h * deep + i
            here = pl.ds(pl.multiple_of(i * rows, 16), rows)
            for block in range(blocks):
                lanes = slice(block * BLOCK, (block + 1) * BLOCK)
                spread_out(block, (flat[here, lanes] * pert[level, :, lanes].astype(F32)).astype(BF16))
            out = along_longitude(level)
            reach = pl.ds(pl.multiple_of(level * HALO, 8), HALO)
            for block in range(blocks):
                lanes = slice(block * BLOCK, (block + 1) * BLOCK)
                value = out[block * rows : (block + 1) * rows]
                band[level, :, lanes] = value.astype(BF16)
                edge_f[0, reach, lanes] = value[0:HALO]
                edge_f[1, reach, lanes] = value[rows - HALO : rows]
            return carry

        lax.fori_loop(0, deep, body, 0)

    def finish(h):
        for i in range(deep):
            level = h * deep + i
            for block in range(blocks):
                back[level, :, block * BLOCK : (block + 1) * BLOCK] = smooth(1, h, level, block)
            lev_copy(1, level).start()

    halves = range(PAIRS)
    groups_of = [range(h * deep, (h + 1) * deep) for h in halves]
    for level in range(levels):
        lev_copy(0, level).wait_recv()
    for h in halves:
        vertical(groups_of[h], outer)
        send_edges(0, h)
    vertical(range(levels), inner_chunks)
    lax.fori_loop(0, levels, build_table, 0)
    load(0).wait()
    for h in halves:
        receive_edges(0, h)
        forward(h)
        sum_level(h, 0)
    site_copy(1 - group).wait_recv()
    for h in halves:
        see(h)
    for which in range(1, max(tree.height[0] for tree in trees)):
        for h in halves:
            sum_level(h, which)
    for h in halves:
        sum_root(h)
    for h in halves:
        adjoint(h)
    for h in halves:
        increments(h)
    store_inc = pltpu.make_async_copy(inc, inc_out, inc_sem)
    store_inc.start()
    lasts = [tree.height[0] for tree in trees]
    for which in range(1, max(lasts)):
        for h in halves:
            if which < lasts[h]:
                gather_level(h, which)
    for h in halves:
        gather_level(h, lasts[h])
        backward(h)
        send_edges(1, h)
    store_inc.wait()
    site_copy(group).wait_send()
    for level in range(levels):
        lev_copy(0, level).wait_send()
    for h in halves:
        for side in range(2):
            halo_copy(0, h, side).wait_send()
        pair_copy(h).wait_send()
        for node in trees[h].nodes[1:]:
            sum_copy(h, node).wait_send()
            gather_copy(h, node, trees[h].parent[node]).wait_send()
    for h in halves:
        receive_edges(1, h)
        finish(h)
    for level in range(levels):
        lev_copy(1, level).wait_recv()

    for level in range(levels):
        lev_copy(1, level).wait_send()
    for h in halves:
        for side in range(2):
            halo_copy(1, h, side).wait_send()


def last_kernel(alpha, near, far, inc, grad_out, inc_out, grad, store_sem, inc_sem):
    levels, rows, cols = alpha.shape
    near_weights, far_weights = vert_weights(lax.axis_index("lev"), levels)
    parts = [pl.ds(16 * i, 16) for i in range(rows // 16)]

    pass_inc = pltpu.make_async_copy(inc, inc_out, inc_sem)
    pass_inc.start()

    def store(i):
        return pltpu.make_async_copy(grad.at[:, parts[i]], grad_out.at[:, parts[i]], store_sem.at[i])

    for i, part in enumerate(parts):
        def step(block, carry):
            lanes = pl.ds(pl.multiple_of(block * BLOCK, BLOCK), BLOCK)
            a = [near[j, part, lanes].astype(F32) for j in range(levels)]
            b = [far[j, part, lanes].astype(F32) for j in range(levels)]
            for level in range(levels):
                grad[level, part, lanes] = alpha[level, part, lanes] + mix(near_weights, far_weights, a, b, level)
            return carry

        lax.fori_loop(0, cols // BLOCK, step, 0)
        store(i).start()
    for i in range(len(parts)):
        store(i).wait()
    pass_inc.wait()


def solution(mesh):
    ring = mesh.shape["member"] // GROUPS
    lat_count, lev_count = mesh.shape["lat"], mesh.shape["lev"]

    def body(alpha_field, perturbation, obs_value, obs_mask, obs_precision, loc_width):
        _, levels, rows, cols = alpha_field.shape
        cell = obs_value.shape[2]
        deep = levels // PAIRS
        pad = round_up(deep * rows, 128)
        packed = packed_rows(GROUPS * cell)
        edges = len(TREES[0])
        vmem = pl.BlockSpec(memory_space=pltpu.VMEM)
        hbm = pl.BlockSpec(memory_space=pltpu.HBM)
        dma = pltpu.SemaphoreType.DMA
        full = (levels, rows, cols)
        alpha = alpha_field[0]
        near, far, increment = pl.pallas_call(
            functools.partial(kernel, ring, lat_count, lev_count),
            out_shape=(
                pltpu.VMEM(full, BF16),
                pltpu.VMEM(full, BF16),
                jax.ShapeDtypeStruct((levels, cell, rows), F32),
            ),
            in_specs=[hbm] * 6,
            out_specs=(vmem, vmem, hbm),
            scratch_shapes=[
                pltpu.VMEM(full, F32),
                pltpu.VMEM(full, BF16),
                pltpu.VMEM((levels, cell, rows), F32),
                pltpu.VMEM((levels, cell, rows), jnp.int32),
                pltpu.SMEM((levels,), F32),
                pltpu.SMEM((levels,), jnp.int32),
                pltpu.VMEM(full, BF16),
                pltpu.VMEM(full, BF16),
                pltpu.VMEM(full, BF16),
                pltpu.VMEM((2, levels * HALO, cols), F32),
                pltpu.VMEM((2, PAIRS, 2, deep * HALO, cols), BF16),
                pltpu.VMEM((2, PAIRS, 2, deep * HALO, cols), BF16),
                pltpu.VMEM((levels, 2 * rows, BLOCK), BF16),
                pltpu.VMEM((levels, cols, BLOCK), BF16),
                pltpu.VMEM((cols // BLOCK * rows, cols), BF16),
                pltpu.VMEM((pad, cols), F32),
                pltpu.VMEM((PAIRS, cols, pad), F32),
                pltpu.VMEM((GROUPS * cell, pad), F32),
                pltpu.VMEM((PAIRS, edges, packed, 128), BF16),
                pltpu.VMEM((PAIRS, edges, packed, 128), BF16),
                pltpu.VMEM((PAIRS, packed, 128), BF16),
                pltpu.VMEM((PAIRS, packed, 128), BF16),
                pltpu.VMEM((GROUPS, PAIRS, 2, cell, pad), F32),
                pltpu.VMEM((PAIRS, packed, 128), F32),
                pltpu.VMEM((PAIRS, 2, packed, 128), F32),
                pltpu.VMEM((PAIRS, ring, packed, 128), BF16),
                pltpu.VMEM((levels, cell, rows), F32),
                dma((5 + levels,)),
                dma((2, levels)), dma((2, levels)),
                dma((2, PAIRS, 2)), dma((2, PAIRS, 2)),
                dma, dma,
                dma((PAIRS, edges)), dma((PAIRS, edges)),
                dma((PAIRS,)), dma((PAIRS,)),
                dma((PAIRS, edges)), dma((PAIRS, edges)),
                dma,
            ],
            compiler_params=pltpu.CompilerParams(
                collective_id=0, has_side_effects=True, vmem_limit_bytes=32 * 1024 * 1024
            ),
            name="envar",
        )(
            *[
                pltpu.with_memory_space_constraint(x, pltpu.HBM)
                for x in (
                    alpha,
                    perturbation[0],
                    obs_value.transpose(0, 2, 1),
                    obs_mask.transpose(0, 2, 1),
                    obs_precision,
                    loc_width,
                )
            ]
        )
        gradient, increment = pl.pallas_call(
            last_kernel,
            out_shape=(
                jax.ShapeDtypeStruct(full, F32),
                jax.ShapeDtypeStruct((levels, cell, rows), F32),
            ),
            in_specs=[vmem, vmem, vmem, hbm],
            out_specs=(hbm, hbm),
            scratch_shapes=[
                pltpu.VMEM(full, F32),
                dma((rows // 16,)),
                dma,
            ],
            compiler_params=pltpu.CompilerParams(vmem_limit_bytes=16 * 1024 * 1024),
            name="vertical",
        )(alpha, near, far, increment)
        return gradient[None], increment.transpose(0, 2, 1)

    return jax.shard_map(
        body,
        mesh=mesh,
        in_specs=(
            P("member", "lev", "lat", None),
            P("member", "lev", "lat", None),
            P("lev", "lat", "member"),
            P("lev", "lat", "member"),
            P("lev"),
            P("lev"),
        ),
        out_specs=(P("member", "lev", "lat", None), P("lev", "lat", "member")),
        check_vma=False,
    )
```

```python
import functools
import math

import jax
import jax.numpy as jnp
from jax import lax
from jax.experimental import pallas as pl
from jax.experimental.pallas import tpu as pltpu
from jax.sharding import PartitionSpec as P

HALO = 24
GROUPS = 2
PAIRS = 2
BLOCK = 256
VERT_SCALE = 2.0
F32 = jnp.float32
BF16 = jnp.bfloat16
MESH = pl.DeviceIdType.MESH

FIRST = [(0, 3), (0, 1), (3, 6), (3, 4), (1, 2), (6, 8), (6, 7), (4, 5)]
SECOND = [(0, 3), (3, 6), (3, 4), (3, 2), (6, 8), (6, 7), (4, 5), (2, 1)]


def both_sides(side, sign):
    return [(sign * p, sign * c) for p, c in side] + [(-sign * p, -sign * c) for p, c in side if c < 8]


TREES = [both_sides(FIRST, 1), both_sides(SECOND, -1)]


class Tree:
    def __init__(self, pairs):
        self.nodes = [0] + [c for _, c in pairs]
        self.index = {c: i for i, (_, c) in enumerate(pairs)}
        self.parent = {c: p for p, c in pairs}
        self.children = {n: [c for p, c in pairs if p == n] for n in self.nodes}
        self.height = {}
        for n in sorted(self.nodes, key=lambda n: -self.depth(n)):
            self.height[n] = 1 + max([self.height[c] for c in self.children[n]], default=-1)

    def depth(self, node):
        return 0 if node == 0 else 1 + self.depth(self.parent[node])


def round_up(value, to):
    return -(-value // to) * to


def vert_weight(diff):
    return 0.5 * math.exp(-diff * diff / (2.0 * VERT_SCALE * VERT_SCALE))


def vert_weights(lev, levels):
    near = [[vert_weight(i - j) for j in range(levels)] for i in range(levels)]
    far = [
        [
            jnp.where(lev == 0, jnp.float32(vert_weight(i - j - levels)), jnp.float32(vert_weight(i - j + levels)))
            for j in range(levels)
        ]
        for i in range(levels)
    ]
    return near, far


def mix(near, far, a, b, i):
    value = near[i][0] * a[0]
    for j in range(1, len(a)):
        value = value + near[i][j] * a[j]
    for j in range(len(b)):
        value = value + far[i][j] * b[j]
    return value


def remainder_rows(chunk):
    return round_up(-(-chunk // 4), 8)


def packed_rows(chunk):
    return chunk + remainder_rows(chunk)


def pack(value):
    chunk = value.shape[0]
    part = remainder_rows(chunk)
    rest = value[:, 128:256]
    tail = rest[0:part]
    for g in range(1, 4):
        piece = rest[g * part : min((g + 1) * part, chunk)]
        if piece.shape[0] == 0:
            continue
        if piece.shape[0] < part:
            piece = jnp.concatenate([piece, jnp.zeros((part - piece.shape[0], 128), value.dtype)], axis=0)
        tail = tail + pltpu.roll(piece, 32 * g, 1)
    parts = [value[:, 0:128], tail]
    left = packed_rows(chunk) - chunk - part
    if left:
        parts.append(jnp.zeros((left, 128), value.dtype))
    return jnp.concatenate(parts, axis=0)


def unpack(value, chunk):
    part = remainder_rows(chunk)
    tail = value[chunk : chunk + part]
    pieces = [tail]
    for g in range(1, 4):
        keep = min(part, chunk - g * part)
        if keep > 0:
            pieces.append(pltpu.roll(tail, 128 - 32 * g, 1)[0:keep])
    return jnp.concatenate([value[0:chunk], jnp.concatenate(pieces, axis=0)], axis=1)


def kernel(
    ring, lat_count, lev_count,
    alpha_in, pert_in, obs_in, mask_in, prec_in, width_in,
    back, far_out, inc_out,
    alpha, pert, obs, mask, prec, width, own, far, band, edge_f, edge, halo, latk, table, rolled, flat, turned,
    mixed, sum_tx, sum_rx, pair_tx, pair_rx, site, total, seen, adj, inc,
    load_sem, lev_send, lev_recv, halo_send, halo_recv, site_send, site_recv,
    sum_send, sum_recv, pair_send, pair_recv, gather_send, gather_recv, inc_sem,
):
    levels, rows, cols = alpha.shape
    blocks = cols // BLOCK
    cell = cols // (ring * GROUPS)
    chunk_rows = GROUPS * cell
    pad = flat.shape[0]
    deep = levels // PAIRS
    used = deep * rows
    trees = [Tree(pairs) for pairs in TREES]

    member = lax.axis_index("member")
    lat = lax.axis_index("lat")
    lev = lax.axis_index("lev")
    z = lax.rem(member, ring)
    group = lax.div(member, ring)

    def place(offset):
        return lax.rem(z + (ring + offset), ring)

    def at(offset):
        return {"member": group * ring + place(offset)}

    pair = {"member": lax.rem(member + ring, ring * GROUPS)}
    south = {"lat": lax.rem(lat + 1, lat_count)}
    north = {"lat": lax.rem(lat + lat_count - 1, lat_count)}
    sibling = {"lev": 1 - lev}

    def remote(src, dst, send, recv, to):
        return pltpu.make_async_remote_copy(
            src_ref=src, dst_ref=dst, send_sem=send, recv_sem=recv, device_id=to, device_id_type=MESH
        )

    def lev_copy(phase, level):
        src, dst = ((own, far), (back, far_out))[phase]
        return remote(src.at[level], dst.at[level], lev_send.at[phase, level], lev_recv.at[phase, level], sibling)

    def halo_copy(phase, h, side):
        return remote(
            edge.at[phase, h, side], halo.at[phase, h, 1 - side],
            halo_send.at[phase, h, side], halo_recv.at[phase, h, 1 - side], (north, south)[side],
        )

    def site_copy(whose):
        return remote(site.at[whose], site.at[whose], site_send, site_recv, pair)

    def sum_copy(h, node):
        i = trees[h].index[node]
        to = at(trees[h].parent[node] - node)
        return remote(sum_tx.at[h, i], sum_rx.at[h, i], sum_send.at[h, i], sum_recv.at[h, i], to)

    def pair_copy(h):
        return remote(pair_tx.at[h], pair_rx.at[h], pair_send.at[h], pair_recv.at[h], pair)

    def gather_copy(h, node, holder):
        i = trees[h].index[node]
        chunk = place(-holder)
        to = at(node - trees[h].parent[node])
        return remote(adj.at[h, chunk], adj.at[h, chunk], gather_send.at[h, i], gather_recv.at[h, i], to)

    barrier = pltpu.get_barrier_semaphore()
    jumps = sorted({s * (p - c) for pairs in TREES for p, c in pairs for s in (1, -1)})
    partners = [sibling, south, north, pair] + [at(jump) for jump in jumps]
    for partner in partners:
        pl.semaphore_signal(barrier, inc=1, device_id=partner, device_id_type=MESH)

    def load(i, level=None):
        if level is None:
            src, dst = ((pert_in, pert), (obs_in, obs), (mask_in, mask), (prec_in, prec), (width_in, width))[i]
        else:
            src, dst = alpha_in.at[level], alpha.at[level]
        return pltpu.make_async_copy(src, dst, load_sem.at[i])

    for level in range(levels):
        load(5 + level, level).start()
    for i in (3, 4, 1, 2, 0):
        load(i).start()

    def round_level(level, carry):
        own[level] = alpha[level].astype(BF16)
        return carry

    for level in range(levels):
        load(5 + level, level).wait()
    lax.fori_loop(0, levels, round_level, 0)
    pl.semaphore_wait(barrier, len(partners))

    for level in range(levels):
        lev_copy(0, level).start()

    for i in (3, 4, 1, 2):
        load(i).wait()

    site[group] = jnp.zeros(site.shape[1:], F32)
    for level in range(levels):
        lanes = slice((level % deep) * rows, (level % deep + 1) * rows)
        site[group, level // deep, 0, :, lanes] = obs[level]
        site[group, level // deep, 1, :, lanes] = mask[level].astype(F32) * prec[level]

    site_copy(group).start()

    def build_latk(level, carry):
        scale = jnp.full((1, 128), width[level].astype(F32), F32) / 3.0
        lane = lax.broadcasted_iota(jnp.int32, (1, 128), 1)
        step = (lane - HALO).astype(F32)
        norm_sq = jnp.sum(
            jnp.where(lane <= 2 * HALO, jnp.exp(-(step * step) / (scale * scale)), 0.0), axis=1, keepdims=True
        )
        scale = scale[:, 0:1]
        row = lax.broadcasted_iota(jnp.int32, (rows, BLOCK), 0)
        col = lax.broadcasted_iota(jnp.int32, (rows, BLOCK), 1)
        top = rows + HALO * lax.rem(level, deep)
        bottom = top + HALO * deep
        is_top = jnp.logical_and(col >= top, col < top + HALO)
        is_bottom = jnp.logical_and(col >= bottom, col < bottom + HALO)
        spot = jnp.where(is_top, col - top - HALO, col)
        spot = jnp.where(is_bottom, col - bottom + rows, spot)
        diff = spot - row
        keep = jnp.logical_or(
            col < rows,
            jnp.logical_or(jnp.logical_and(is_top, lat > 0), jnp.logical_and(is_bottom, lat < lat_count - 1)),
        )
        keep = jnp.logical_and(keep, jnp.abs(diff) <= HALO)
        dist = diff.astype(F32)
        weight = jnp.exp(-(dist * dist) / (2.0 * scale * scale)) / jnp.sqrt(norm_sq)
        weight = jnp.where(keep, weight, 0.0)
        high = weight.astype(BF16)
        latk[level, 0:rows] = high
        latk[level, rows : 2 * rows] = (weight - high.astype(F32)).astype(BF16)
        return carry

    lax.fori_loop(0, levels, build_latk, 0)

    def build_table(level, carry):
        scale = jnp.full((1, 128), width[level].astype(F32), F32)[:, 0:1]
        square = scale * scale
        spot = lax.broadcasted_iota(jnp.int32, (1, cols), 1)
        cycle = jnp.minimum(spot, cols - spot).astype(F32)
        norm_sq = jnp.sum(jnp.exp(-(cycle * cycle) / square), axis=1, keepdims=True)
        inverse = 1.0 / jnp.sqrt(norm_sq)
        factor = -1.0 / (2.0 * square)
        step = 64

        def some(i, inner):
            row = lax.broadcasted_iota(jnp.int32, (step, BLOCK), 0) + i * step
            col = lax.broadcasted_iota(jnp.int32, (step, BLOCK), 1)
            diff = jnp.abs(row - col)
            dist = jnp.minimum(diff, cols - diff).astype(F32)
            table[level, pl.ds(pl.multiple_of(i * step, step), step)] = (
                jnp.exp(dist * dist * factor) * inverse
            ).astype(BF16)
            return inner

        return lax.fori_loop(0, cols // step, some, carry)

    for h in range(PAIRS):
        turned[h, :, 128:pad] = jnp.zeros((cols, pad - 128), F32)

    near_weights, far_weights = vert_weights(lev, levels)
    row_chunks = list(range(rows // 16))
    outer = [c for c in row_chunks if 16 * c < HALO or 16 * c + 16 > rows - HALO]
    inner_chunks = [c for c in row_chunks if c not in outer]

    def lane_loop(body):
        def step(block, carry):
            body(pl.ds(pl.multiple_of(block * BLOCK, BLOCK), BLOCK))
            return carry

        lax.fori_loop(0, blocks, step, 0)

    def vertical(outs, chunks):
        def body(lanes):
            for chunk in chunks:
                first = 16 * chunk
                part = slice(first, first + 16)
                a = [own[j, part, lanes].astype(F32) for j in range(levels)]
                b = [far[j, part, lanes].astype(F32) for j in range(levels)]
                for i in outs:
                    value = mix(near_weights, far_weights, a, b, i)
                    band[i, part, lanes] = value.astype(BF16)
                    top = min(HALO, first + 16) - first
                    if top > 0:
                        edge_f[0, HALO * i + first : HALO * i + first + top, lanes] = value[0:top]
                    skip = max(0, rows - HALO - first)
                    if skip < 16:
                        start = HALO * i + first + skip - (rows - HALO)
                        edge_f[1, start : start + 16 - skip, lanes] = value[skip:16]

        lane_loop(body)

    def send_edges(phase, h):
        def body(lanes):
            for side in range(2):
                part = slice(h * deep * HALO, (h + 1) * deep * HALO)
                edge[phase, h, side, :, lanes] = edge_f[side, part, lanes].astype(BF16)

        lane_loop(body)
        for side in range(2):
            halo_copy(phase, h, side).start()

    def receive_edges(phase, h):
        for side in range(2):
            halo_copy(phase, h, side).wait_recv()

    def smooth(phase, h, level, block):
        lanes = slice(block * BLOCK, (block + 1) * BLOCK)
        spare = BLOCK - rows - 2 * deep * HALO
        field = jnp.concatenate(
            [band[level, :, lanes], halo[phase, h, 0, :, lanes], halo[phase, h, 1, :, lanes], jnp.zeros((spare, BLOCK), BF16)],
            axis=0,
        )
        both = jnp.dot(latk[level], field, preferred_element_type=F32)
        return (both[0:rows] + both[rows : 2 * rows]).astype(BF16)

    def spread_out(block, value):
        for turn in range(blocks):
            start = ((block - turn) % blocks) * BLOCK
            rolled[turn * rows : (turn + 1) * rows, start : start + BLOCK] = value

    def along_longitude(level):
        return jnp.dot(rolled[...], table[level], preferred_element_type=F32)

    def split_rows(chunk):
        return [pl.ds(pl.multiple_of(g * (cols // GROUPS) + chunk * cell, 8), cell) for g in range(GROUPS)]

    def forward(h):
        def body(i, carry):
            level = h * deep + i
            for block in range(blocks):
                spread_out(block, smooth(0, h, level, block))
            out = along_longitude(level)
            here = pl.ds(pl.multiple_of(i * rows, 16), rows)
            for block in range(blocks):
                lanes = slice(block * BLOCK, (block + 1) * BLOCK)
                flat[here, lanes] = out[block * rows : (block + 1) * rows] * pert[level, :, lanes].astype(F32)
            return carry

        lax.fori_loop(0, deep, body, 0)

        def turn(i, carry):
            part = pl.ds(pl.multiple_of(i * 128, 128), 128)
            turned[h, part, 0:128] = flat[0:128, part].T
            turned[h, part, 128:used] = flat[128:used, part].T
            return carry

        lax.fori_loop(0, cols // 128, turn, 0)

    def sum_at(h, node):
        value = pack(jnp.concatenate([turned[h, part, :] for part in split_rows(place(-node))], axis=0))
        for child in trees[h].children[node]:
            sum_copy(h, child).wait_recv()
            value = value + sum_rx[h, trees[h].index[child]].astype(F32)
        return value

    def sum_level(h, which):
        for node in trees[h].nodes[1:]:
            if trees[h].height[node] == which:
                sum_tx[h, trees[h].index[node]] = sum_at(h, node).astype(BF16)
                sum_copy(h, node).start()

    def sum_root(h):
        value = sum_at(h, 0)
        total[h] = value
        pair_tx[h] = value.astype(BF16)
        pair_copy(h).start()

    def see(h):
        for kind in range(2):
            both = jnp.concatenate([site[g, h, kind] for g in range(GROUPS)], axis=0)
            seen[h, kind] = pack(both)

    def start_gather(h, node):
        for child in trees[h].children[node]:
            gather_copy(h, child, node).start()

    def adjoint(h):
        pair_copy(h).wait_recv()
        summed = total[h] + pair_rx[h].astype(F32)
        adj[h, z] = (seen[h, 1] * (summed - seen[h, 0])).astype(BF16)
        start_gather(h, 0)
        total[h] = summed
        open_up(h, z)

    def open_up(h, chunk):
        value = unpack(adj[h, chunk].astype(F32), chunk_rows)
        for g, part in enumerate(split_rows(chunk)):
            turned[h, part, :] = value[g * cell : (g + 1) * cell]

    def gather_level(h, which):
        here = [n for n in trees[h].nodes if trees[h].depth(n) == which]
        for node in here:
            gather_copy(h, node, node).wait_recv()
            start_gather(h, node)
            if not trees[h].children[node]:
                open_up(h, place(-node))
        for node in here:
            if trees[h].children[node]:
                open_up(h, place(-node))

    def increments(h):
        value = unpack(total[h], chunk_rows)
        mixed[...] = value
        mine = mixed[pl.ds(pl.multiple_of(group * cell, 8), cell), :]
        for i in range(deep):
            inc[h * deep + i] = mine[:, i * rows : (i + 1) * rows]

    def backward(h):
        def turn(i, carry):
            part = pl.ds(pl.multiple_of(i * 128, 128), 128)
            flat[0:128, part] = turned[h, part, 0:128].T
            flat[128:used, part] = turned[h, part, 128:used].T
            return carry

        lax.fori_loop(0, cols // 128, turn, 0)

        def body(i, carry):
            level = h * deep + i
            here = pl.ds(pl.multiple_of(i * rows, 16), rows)
            for block in range(blocks):
                lanes = slice(block * BLOCK, (block + 1) * BLOCK)
                spread_out(block, (flat[here, lanes] * pert[level, :, lanes].astype(F32)).astype(BF16))
            out = along_longitude(level)
            reach = pl.ds(pl.multiple_of(level * HALO, 8), HALO)
            for block in range(blocks):
                lanes = slice(block * BLOCK, (block + 1) * BLOCK)
                value = out[block * rows : (block + 1) * rows]
                band[level, :, lanes] = value.astype(BF16)
                edge_f[0, reach, lanes] = value[0:HALO]
                edge_f[1, reach, lanes] = value[rows - HALO : rows]
            return carry

        lax.fori_loop(0, deep, body, 0)

    def finish(h):
        for i in range(deep):
            level = h * deep + i
            for block in range(blocks):
                back[level, :, block * BLOCK : (block + 1) * BLOCK] = smooth(1, h, level, block)
            lev_copy(1, level).start()

    halves = range(PAIRS)
    groups_of = [range(h * deep, (h + 1) * deep) for h in halves]
    lax.fori_loop(0, 1, build_table, 0)
    for level in range(levels):
        lev_copy(0, level).wait_recv()
    for h in halves:
        vertical(groups_of[h], outer)
        send_edges(0, h)
    vertical(range(levels), inner_chunks)
    lax.fori_loop(1, levels, build_table, 0)
    load(0).wait()
    for h in halves:
        receive_edges(0, h)
        forward(h)
        sum_level(h, 0)
    site_copy(1 - group).wait_recv()
    for h in halves:
        see(h)
    for which in range(1, max(tree.height[0] for tree in trees)):
        for h in halves:
            sum_level(h, which)
    for h in halves:
        sum_root(h)
    for h in halves:
        adjoint(h)
    for h in halves:
        increments(h)
    store_inc = pltpu.make_async_copy(inc, inc_out, inc_sem)
    store_inc.start()
    lasts = [tree.height[0] for tree in trees]
    for which in range(1, max(lasts)):
        for h in halves:
            if which < lasts[h]:
                gather_level(h, which)
    for h in halves:
        gather_level(h, lasts[h])
        backward(h)
        send_edges(1, h)
    store_inc.wait()
    site_copy(group).wait_send()
    for level in range(levels):
        lev_copy(0, level).wait_send()
    for h in halves:
        for side in range(2):
            halo_copy(0, h, side).wait_send()
        pair_copy(h).wait_send()
        for node in trees[h].nodes[1:]:
            sum_copy(h, node).wait_send()
            gather_copy(h, node, trees[h].parent[node]).wait_send()
    for h in halves:
        receive_edges(1, h)
        finish(h)
    for level in range(levels):
        lev_copy(1, level).wait_recv()

    for level in range(levels):
        lev_copy(1, level).wait_send()
    for h in halves:
        for side in range(2):
            halo_copy(1, h, side).wait_send()


def last_kernel(alpha, near, far, inc, grad_out, inc_out, grad, store_sem, inc_sem):
    levels, rows, cols = alpha.shape
    near_weights, far_weights = vert_weights(lax.axis_index("lev"), levels)
    parts = [pl.ds(16 * i, 16) for i in range(rows // 16)]

    pass_inc = pltpu.make_async_copy(inc, inc_out, inc_sem)
    pass_inc.start()

    def store(i):
        return pltpu.make_async_copy(grad.at[:, parts[i]], grad_out.at[:, parts[i]], store_sem.at[i])

    for i, part in enumerate(parts):
        def step(block, carry):
            lanes = pl.ds(pl.multiple_of(block * BLOCK, BLOCK), BLOCK)
            a = [near[j, part, lanes].astype(F32) for j in range(levels)]
            b = [far[j, part, lanes].astype(F32) for j in range(levels)]
            for level in range(levels):
                grad[level, part, lanes] = alpha[level, part, lanes] + mix(near_weights, far_weights, a, b, level)
            return carry

        lax.fori_loop(0, cols // BLOCK, step, 0)
        store(i).start()
    for i in range(len(parts)):
        store(i).wait()
    pass_inc.wait()


def solution(mesh):
    ring = mesh.shape["member"] // GROUPS
    lat_count, lev_count = mesh.shape["lat"], mesh.shape["lev"]

    def body(alpha_field, perturbation, obs_value, obs_mask, obs_precision, loc_width):
        _, levels, rows, cols = alpha_field.shape
        cell = obs_value.shape[2]
        deep = levels // PAIRS
        pad = round_up(deep * rows, 128)
        packed = packed_rows(GROUPS * cell)
        edges = len(TREES[0])
        vmem = pl.BlockSpec(memory_space=pltpu.VMEM)
        hbm = pl.BlockSpec(memory_space=pltpu.HBM)
        dma = pltpu.SemaphoreType.DMA
        full = (levels, rows, cols)
        alpha = alpha_field[0]
        near, far, increment = pl.pallas_call(
            functools.partial(kernel, ring, lat_count, lev_count),
            out_shape=(
                pltpu.VMEM(full, BF16),
                pltpu.VMEM(full, BF16),
                jax.ShapeDtypeStruct((levels, cell, rows), F32),
            ),
            in_specs=[hbm] * 6,
            out_specs=(vmem, vmem, hbm),
            scratch_shapes=[
                pltpu.VMEM(full, F32),
                pltpu.VMEM(full, BF16),
                pltpu.VMEM((levels, cell, rows), F32),
                pltpu.VMEM((levels, cell, rows), jnp.int32),
                pltpu.SMEM((levels,), F32),
                pltpu.SMEM((levels,), jnp.int32),
                pltpu.VMEM(full, BF16),
                pltpu.VMEM(full, BF16),
                pltpu.VMEM(full, BF16),
                pltpu.VMEM((2, levels * HALO, cols), F32),
                pltpu.VMEM((2, PAIRS, 2, deep * HALO, cols), BF16),
                pltpu.VMEM((2, PAIRS, 2, deep * HALO, cols), BF16),
                pltpu.VMEM((levels, 2 * rows, BLOCK), BF16),
                pltpu.VMEM((levels, cols, BLOCK), BF16),
                pltpu.VMEM((cols // BLOCK * rows, cols), BF16),
                pltpu.VMEM((pad, cols), F32),
                pltpu.VMEM((PAIRS, cols, pad), F32),
                pltpu.VMEM((GROUPS * cell, pad), F32),
                pltpu.VMEM((PAIRS, edges, packed, 128), BF16),
                pltpu.VMEM((PAIRS, edges, packed, 128), BF16),
                pltpu.VMEM((PAIRS, packed, 128), BF16),
                pltpu.VMEM((PAIRS, packed, 128), BF16),
                pltpu.VMEM((GROUPS, PAIRS, 2, cell, pad), F32),
                pltpu.VMEM((PAIRS, packed, 128), F32),
                pltpu.VMEM((PAIRS, 2, packed, 128), F32),
                pltpu.VMEM((PAIRS, ring, packed, 128), BF16),
                pltpu.VMEM((levels, cell, rows), F32),
                dma((5 + levels,)),
                dma((2, levels)), dma((2, levels)),
                dma((2, PAIRS, 2)), dma((2, PAIRS, 2)),
                dma, dma,
                dma((PAIRS, edges)), dma((PAIRS, edges)),
                dma((PAIRS,)), dma((PAIRS,)),
                dma((PAIRS, edges)), dma((PAIRS, edges)),
                dma,
            ],
            compiler_params=pltpu.CompilerParams(
                collective_id=0, has_side_effects=True, vmem_limit_bytes=32 * 1024 * 1024
            ),
            name="envar",
        )(
            *[
                pltpu.with_memory_space_constraint(x, pltpu.HBM)
                for x in (
                    alpha,
                    perturbation[0],
                    obs_value.transpose(0, 2, 1),
                    obs_mask.transpose(0, 2, 1),
                    obs_precision,
                    loc_width,
                )
            ]
        )
        gradient, increment = pl.pallas_call(
            last_kernel,
            out_shape=(
                jax.ShapeDtypeStruct(full, F32),
                jax.ShapeDtypeStruct((levels, cell, rows), F32),
            ),
            in_specs=[vmem, vmem, vmem, hbm],
            out_specs=(hbm, hbm),
            scratch_shapes=[
                pltpu.VMEM(full, F32),
                dma((rows // 16,)),
                dma,
            ],
            compiler_params=pltpu.CompilerParams(vmem_limit_bytes=16 * 1024 * 1024),
            name="vertical",
        )(alpha, near, far, increment)
        return gradient[None], increment.transpose(0, 2, 1)

    return jax.shard_map(
        body,
        mesh=mesh,
        in_specs=(
            P("member", "lev", "lat", None),
            P("member", "lev", "lat", None),
            P("lev", "lat", "member"),
            P("lev", "lat", "member"),
            P("lev"),
            P("lev"),
        ),
        out_specs=(P("member", "lev", "lat", None), P("lev", "lat", "member")),
        check_vma=False,
    )
```
